512 devices in a mesh: bins: 64 (over y, z_hi, x), view: 8 (over z_lo, core).
Axes of the slice: x: 4, y: 8, z: 8 (z_hi: 2, z_lo: 4; z = z_hi * 4 + z_lo), core: 2. Of those that a mesh axis runs over, the one named last changes fastest.
Arguments:
- latent_shocks: bfloat16 [65536, 128], P('bins'), may hold values from -6 to 6
- shock_direction: bfloat16 [65536, 128], P('bins'), may hold values from -6 to 6
- coupling_matrix: bfloat16 [5120, 128], P('view'), may hold values from -0.5 to 0.5
- signal_assay_map: int32 [5120], P('view'), may hold values from 0 to 7
- assay_depth_shift: float32 [8, 65536], P(None, 'bins'), may hold values from -3 to -1
- persistence_span: float32 [128], replicated, may hold values from 30 to 131072
- carry_weight: float32 [65536], P('bins'), as said below
- segment_beginnings: int32 [3], replicated, may hold values from 1 to 65535, as said below
Outputs:
- curvature_product: float32 [65536, 128], P('bins')
The draws below stay inside these ranges and needn't reach their ends.
Inputs may be any that keep to these rules, and one draw needn't show every extreme that they name: `segment_beginnings`: 3 distinct bins; the first is 1 and the last is 65535. `carry_weight`: most entries equal 1; the others lie between 0.5 and 0.8.
All inputs are finite; a program needn't handle non-finite values.
Results may differ from the reference program's by a relative error of at most 0.0003.
Values sent between devices are 32-bit elements; how exact they have to be, the bound alone decides.
No kernel may reach another device: no remote copies, remote signals or barrier semaphores. Data moves between devices by JAX's collectives and lax.ppermute only.
A program may use at most 128 MiB of HBM per device.

```python
import jax
import jax.numpy as jnp
from jax import lax

TRACKS = 5120
K = 128
NVIEW = 8
NCHR = 3
BINS = 65536


def draw_persistence_span(key, part):
    key_slow = jax.random.fold_in(key, 11)
    key_pick = jax.random.fold_in(key, 12)
    key_ends = jax.random.fold_in(key, 13)
    spread = jax.random.uniform(key_pick, (K,), jnp.float32)
    slow_mask = jax.random.uniform(key_slow, (K,), jnp.float32) < 0.5
    slow_mem = jnp.exp(jnp.log(BINS * 0.5) + spread * jnp.log(4.0))
    fast_mem = jnp.exp(jnp.log(30.0) + spread * jnp.log(BINS / 60.0))
    values = jnp.where(slow_mask, slow_mem, fast_mem)
    order = jax.random.permutation(key_ends, K)
    index = jnp.arange(K)
    values = jnp.where(index == order[0], 30.0, values)
    values = jnp.where(index == order[1], 2.0 * BINS, values)
    return values.astype(jnp.float32)


def draw_carry_weight(key, part):
    key_where = jax.random.fold_in(key, 21)
    key_value = jax.random.fold_in(key, 22)
    picked = jax.random.randint(key_where, (BINS,), 0, BINS) < 16
    amount = jax.random.uniform(key_value, (BINS,), jnp.float32, 0.5, 0.8)
    return jnp.where(picked, amount, 1.0).astype(jnp.float32)


def draw_segment_beginnings(key, part):
    key_perm = jax.random.fold_in(key, 31)
    middle = jax.random.permutation(key_perm, BINS - 3)[:NCHR - 2] + 2
    first = jnp.ones((1,), jnp.int32)
    final = jnp.full((1,), BINS - 1, jnp.int32)
    return jnp.concatenate([first, middle.astype(jnp.int32), final]).astype(jnp.int32)


def with_ends(values, key, smallest, largest):
    longest = values.shape.index(max(values.shape))
    spots = []
    for shift in (0, 1):
        where = [jax.random.randint(jax.random.fold_in(key, axis), (), 0, length) for axis, length in enumerate(values.shape)]
        where[longest] = (where[longest] + shift) % values.shape[longest]
        spots.append(tuple(where))
    return values.at[spots[0]].set(smallest).at[spots[1]].set(largest)


def shard_levels(own_key, extent, pieces, smallest, high):
    factor_of = 1.0
    for position, blocks in pieces:
        heights = jax.random.uniform(jax.random.fold_in(jax.random.fold_in(own_key, 6), position), (blocks,), jnp.float32, smallest / len(pieces), high / len(pieces))
        factor_of = factor_of * jnp.repeat(jnp.exp(heights), extent[position] // blocks).reshape((-1,) + (1,) * (len(extent) - 1 - position))
    return factor_of


def scatter_about(rng, extent, deviation, reach, pieces=(), kind=jnp.bfloat16):
    factor_of = shard_levels(rng, extent, pieces, -0.22, 0.18) if pieces else 1.0
    values = jax.random.normal(rng, extent, jnp.float32) * deviation * factor_of
    return jnp.minimum(jnp.maximum(values, -reach), reach).astype(kind)


def setup_inputs(seed: int = 0) -> dict:
    arg_keys = jax.random.split(jax.random.key(seed), 9)
    latent_shocks = scatter_about(arg_keys[0], (BINS, K), 1.0, 6.0, ((0, 64),))
    shock_direction = scatter_about(arg_keys[1], (BINS, K), 1.0, 6.0, ((0, 64),))
    coupling_matrix = scatter_about(arg_keys[2], (TRACKS, K), K ** -0.5, 0.5, ((0, 8),))
    signal_assay_map = with_ends(jax.random.randint(arg_keys[3], (TRACKS,), 0, NVIEW), jax.random.fold_in(arg_keys[3], 1), 0, NVIEW - 1).astype(jnp.int32)
    assay_depth_shift = jnp.clip(-3.0 + 2.0 * jax.random.uniform(arg_keys[4], (NVIEW, BINS), jnp.float32) ** shard_levels(arg_keys[4], (NVIEW, BINS), ((1, 64),), -0.2, 0.2), -3.0, -1.0)
    persistence_span = draw_persistence_span(jax.random.fold_in(arg_keys[8], 71), 0)
    carry_weight = draw_carry_weight(jax.random.fold_in(arg_keys[8], 71), 0)
    segment_beginnings = draw_segment_beginnings(jax.random.fold_in(arg_keys[8], 71), 0)
    return dict(latent_shocks=latent_shocks, shock_direction=shock_direction, coupling_matrix=coupling_matrix, signal_assay_map=signal_assay_map, assay_depth_shift=assay_depth_shift, persistence_span=persistence_span, carry_weight=carry_weight, segment_beginnings=segment_beginnings)


def compose(early, late):
    head = early[0] * late[0]
    return (head,) + tuple((late[0] * older + newer for older, newer in zip(early[1:], late[1:])))

def shrink_times_boost(persistence_span, carry_weight, segment_beginnings, topmost_line):
    discard_multiplier = 1.0 / persistence_span
    line_indices = topmost_line + jnp.arange(carry_weight.shape[0], dtype=jnp.int32)
    is_start = jnp.any(line_indices[:, None] == segment_beginnings[None, :].astype(jnp.int32), axis=1)
    keeping_fraction = (1.0 - discard_multiplier)[None, :] * carry_weight[:, None]
    shrink_multiplier = jnp.where(is_start[:, None], jnp.zeros_like(keeping_fraction), keeping_fraction)
    return (shrink_multiplier, jnp.sqrt(discard_multiplier * (2.0 - discard_multiplier)))

def weigh_block(latent_b, moved_b, offset_b, coupling_matrix, member):
    contract = (((1,), (1,)), ((), ()))
    log_rate = lax.dot_general(latent_b, coupling_matrix, contract, preferred_element_type=jnp.float32)
    log_rate = log_rate + lax.dot_general(offset_b, member, (((0,), (0,)), ((), ())), precision=lax.Precision.HIGHEST)
    along = lax.dot_general(moved_b, coupling_matrix, contract, preferred_element_type=jnp.float32)
    weighted = (jnp.exp(log_rate) * along).astype(jnp.bfloat16)
    return jnp.dot(weighted, coupling_matrix, preferred_element_type=jnp.float32)

def track_terms(latent, moved, assay_depth_shift, coupling_matrix, member):
    row_count = latent.shape[0]
    block = 1024 if row_count % 1024 == 0 else row_count
    nblock = row_count // block
    latent_b = latent.astype(jnp.bfloat16).reshape(nblock, block, latent.shape[1])
    moved_b = moved.astype(jnp.bfloat16).reshape(nblock, block, moved.shape[1])
    offset_b = assay_depth_shift.reshape(assay_depth_shift.shape[0], nblock, block).transpose(1, 0, 2)
    result = lax.map(lambda items: weigh_block(items[0], items[1], items[2], coupling_matrix, member), (latent_b, moved_b, offset_b))
    return result.reshape(row_count, latent.shape[1])

def reference(latent_shocks, shock_direction, coupling_matrix, signal_assay_map, assay_depth_shift, persistence_span, carry_weight, segment_beginnings):
    shrink_multiplier, boost_multiplier = shrink_times_boost(persistence_span, carry_weight, segment_beginnings, 0)
    prod_run, latent, moved = lax.associative_scan(compose, (shrink_multiplier, boost_multiplier[None, :] * latent_shocks.astype(jnp.float32), boost_multiplier[None, :] * shock_direction.astype(jnp.float32)))
    member = (signal_assay_map[None, :] == jnp.arange(assay_depth_shift.shape[0], dtype=jnp.int32)[:, None]).astype(jnp.float32)
    pulled = track_terms(latent, moved, assay_depth_shift, coupling_matrix, member)
    flip_m, flip_p = lax.associative_scan(compose, (jnp.flip(shrink_multiplier, 0), jnp.flip(shrink_multiplier * pulled, 0)))
    carried = jnp.flip(flip_p, 0)
    p_next = jnp.concatenate([carried[1:], jnp.zeros((1, carried.shape[1]), jnp.float32)], axis=0)
    adjoint = pulled + p_next
    return boost_multiplier[None, :] * adjoint + shock_direction.astype(jnp.float32)
```

```python
import jax
import jax.numpy as jnp
from jax import lax
from jax.experimental import pallas as pl
from jax.experimental.pallas import tpu as pltpu
from jax.sharding import Mesh, PartitionSpec as P

ROWS, K, CHUNKS, STEPS = 1024, 128, 8, 128
PEERS, NVIEW, TRACKS = 64, 8, 640
BLOCK = 256
PART = STEPS + 8
BINS, VIEW = ("y", "zh", "x"), ("zl", "core")
VMEM, SMEM = pltpu.VMEM, pltpu.SMEM


def spec(space):
    return pl.BlockSpec(memory_space=space)


def call(body, ins, outs, scratch=()):
    return pl.pallas_call(
        body,
        in_specs=[spec(s) for s in ins],
        out_specs=[spec(VMEM) for _ in outs],
        out_shape=[jax.ShapeDtypeStruct(shape, dtype) for shape, dtype in outs],
        scratch_shapes=list(scratch),
        compiler_params=pltpu.CompilerParams(vmem_limit_bytes=48 * 1024 * 1024),
    )


def factors(here_ref, begin_ref, span_ref, carry_ref):
    forget = 1.0 / span_ref[...]
    at = (
        here_ref[0] * ROWS
        + lax.broadcasted_iota(jnp.int32, (CHUNKS, STEPS), 0) * STEPS
        + lax.broadcasted_iota(jnp.int32, (CHUNKS, STEPS), 1)
    )
    begins = (at == begin_ref[0]) | (at == begin_ref[1]) | (at == begin_ref[2])
    carry = jnp.where(begins, 0.0, carry_ref[...])
    return 1.0 - forget, jnp.sqrt(forget * (2.0 - forget)), carry


def decay_at(keep, carry, i):
    return jnp.broadcast_to(carry[:, i : i + 1], (CHUNKS, K)) * keep


def rows(ref, i, stride=STEPS):
    return ref[pl.ds(i, CHUNKS, stride=stride), :]


def ends_kernel(here, begin, span, carry_ref, x, d, chunk, sent, xs, ds):
    keep, gain, carry = factors(here, begin, span, carry_ref)
    xs[...] = gain * x[...].astype(jnp.float32)
    ds[...] = gain * d[...].astype(jnp.float32)
    z, v, m = rows(xs, 0), rows(ds, 0), decay_at(keep, carry, 0)
    for i in range(1, STEPS):
        decay = decay_at(keep, carry, i)
        z = decay * z + rows(xs, i)
        v = decay * v + rows(ds, i)
        m = decay * m
    chunk[0] = m
    chunk[1] = z
    chunk[2] = v
    mt, zt, vt = m[0:1], z[0:1], v[0:1]
    for j in range(1, CHUNKS):
        mj = m[j : j + 1]
        mt, zt, vt = mj * mt, mj * zt + z[j : j + 1], mj * vt + v[j : j + 1]
    sent[...] = jnp.broadcast_to(jnp.concatenate([mt, zt, vt], axis=0)[None], sent.shape)


def prepare_kernel(shift, assay, coupling, shift_t, coupling_t):
    s = shift[...]
    hi = s.astype(jnp.bfloat16).astype(jnp.float32)
    mid = (s - hi).astype(jnp.bfloat16).astype(jnp.float32)
    low = s - hi - mid
    blank = jnp.zeros((K - 3 * NVIEW, ROWS), jnp.float32)
    shift_t[...] = jnp.concatenate([hi, mid, low, blank], axis=0).T.astype(jnp.bfloat16)
    member = (
        assay[...] == lax.broadcasted_iota(jnp.int32, (NVIEW, TRACKS), 0)
    ).astype(jnp.float32)
    blank = jnp.zeros((K - 3 * NVIEW, TRACKS), jnp.float32)
    coupling_t[0:K] = coupling[...].astype(jnp.float32).T.astype(jnp.bfloat16)
    coupling_t[K : 2 * K] = jnp.concatenate([member, member, member, blank], axis=0).astype(
        jnp.bfloat16
    )


def tracks_kernel(
    here, begin, span, carry_ref, x, d, chunk, got, shift_t, coupling_t, coupling,
    parts, sent, xs, ds, pulled,
):
    keep, gain, carry = factors(here, begin, span, carry_ref)
    xs[...] = gain * x[...].astype(jnp.float32)
    ds[...] = gain * d[...].astype(jnp.float32)
    ez = jnp.zeros((1, K), jnp.float32)
    ev = jnp.zeros((1, K), jnp.float32)
    for e in range(PEERS - 1):
        m, z, v = got[e, 0:1, :], got[e, 1:2, :], got[e, 2:3, :]
        earlier = e < here[0]
        ez = jnp.where(earlier, m * ez + z, ez)
        ev = jnp.where(earlier, m * ev + v, ev)
    zs, vs = [ez], [ev]
    for j in range(CHUNKS - 1):
        m = chunk[0, j : j + 1, :]
        zs.append(m * zs[-1] + chunk[1, j : j + 1, :])
        vs.append(m * vs[-1] + chunk[2, j : j + 1, :])
    z, v = jnp.concatenate(zs, axis=0), jnp.concatenate(vs, axis=0)
    for i in range(STEPS):
        decay = decay_at(keep, carry, i)
        z = decay * z + rows(xs, i)
        v = decay * v + rows(ds, i)
        xs[pl.ds(i, CHUNKS, stride=STEPS), :] = z
        ds[pl.ds(i, CHUNKS, stride=STEPS), :] = v
    for b in range(ROWS // BLOCK):
        at = pl.ds(b * BLOCK, BLOCK)
        latent = xs[at, :].astype(jnp.bfloat16)
        moved = ds[at, :].astype(jnp.bfloat16)
        log_rate = jnp.dot(
            jnp.concatenate([latent, shift_t[at, :]], axis=1),
            coupling_t[...],
            preferred_element_type=jnp.float32,
        )
        along = jnp.dot(moved, coupling_t[0:K, :], preferred_element_type=jnp.float32)
        weighted = (jnp.exp(log_rate) * along).astype(jnp.bfloat16)
        pulled[at, :] = jnp.dot(weighted, coupling[...], preferred_element_type=jnp.float32)
    for j in range(CHUNKS):
        parts[(j % 4) * 2 + j // 4] = pulled[pl.ds(j * STEPS, STEPS), :]
    r = jnp.zeros((CHUNKS, K), jnp.float32)
    for i in reversed(range(STEPS)):
        r = decay_at(keep, carry, i) * (rows(pulled, i) + r)
    total = r[CHUNKS - 1 : CHUNKS]
    for j in reversed(range(CHUNKS - 1)):
        total = chunk[0, j : j + 1, :] * total + r[j : j + 1]
    sent[...] = jnp.broadcast_to(total[None], sent.shape)


def sum_kernel(here, got, late, parts, out):
    total = parts[0]
    for j in range(1, NVIEW):
        total = total + parts[j]
    entry = jnp.zeros((1, K), jnp.float32)
    for e in reversed(range(1, PEERS)):
        entry = jnp.where(e > here[0], got[e, 0:1, :] * entry + late[e], entry)
    tail = jnp.concatenate([entry, jnp.zeros((PART - STEPS - 1, K), jnp.float32)], axis=0)
    for j in range(4):
        out[j, 0:STEPS, :] = total
        out[j, STEPS:PART, :] = tail


def finish_kernel(here, begin, span, carry_ref, d, chunk, parts, out, adjoint):
    keep, gain, carry = factors(here, begin, span, carry_ref)
    r = jnp.zeros((CHUNKS, K), jnp.float32)
    for i in reversed(range(STEPS)):
        r = decay_at(keep, carry, i) * (rows(parts, i, PART) + r)
    entry = parts[STEPS : STEPS + 1, :]
    for j in range(1, CHUNKS):
        entry = entry + parts[j * PART + STEPS : j * PART + STEPS + 1, :]
    entries = [entry]
    for j in reversed(range(1, CHUNKS)):
        entries.append(chunk[0, j : j + 1, :] * entries[-1] + r[j : j + 1])
    r = jnp.concatenate(entries[::-1], axis=0)
    for i in reversed(range(STEPS)):
        a = rows(parts, i, PART) + r
        adjoint[pl.ds(i, CHUNKS, stride=STEPS), :] = a
        r = decay_at(keep, carry, i) * a
    out[...] = gain * adjoint[...] + d[...].astype(jnp.float32)


def local(x, d, coupling, assay, shift, span, carry, begin):
    f32, bf16 = jnp.float32, jnp.bfloat16
    here = lax.axis_index(BINS)[None]
    span = span.reshape(1, K)
    carry = carry.reshape(CHUNKS, STEPS)
    assay = assay.reshape(1, TRACKS)
    wide = VMEM((ROWS, K), f32)
    head = (here, begin, span, carry)
    heads = [SMEM, SMEM, VMEM, VMEM]
    chunk, sent = call(
        ends_kernel, heads + [VMEM] * 2, [((3, CHUNKS, K), f32), ((PEERS, 3, K), f32)], [wide] * 2
    )(*head, x, d)
    got = lax.all_to_all(sent, BINS, 0, 0, tiled=True)
    shift_t, coupling_t = call(
        prepare_kernel, [VMEM] * 3, [((ROWS, K), bf16), ((2 * K, TRACKS), bf16)]
    )(shift, assay, coupling)
    parts, sent = call(
        tracks_kernel,
        heads + [VMEM] * 7,
        [((NVIEW, STEPS, K), f32), ((PEERS, 1, K), f32)],
        [wide] * 3,
    )(*head, x, d, chunk, got, shift_t, coupling_t, coupling)
    late = lax.all_to_all(sent, BINS, 0, 0, tiled=True)
    parts = lax.all_to_all(parts, VIEW, 0, 0, tiled=True)
    (mine,) = call(sum_kernel, [SMEM] + [VMEM] * 3, [((4, PART, K), f32)])(here, got, late, parts)
    column = lax.all_to_all(mine, "zl", 0, 0, tiled=True)
    parts = lax.all_gather(column, "core").reshape(CHUNKS * PART, K)
    (out,) = call(finish_kernel, heads + [VMEM] * 3, [((ROWS, K), f32)], [wide])(
        *head, d, chunk, parts
    )
    return out


def solution(mesh):
    fine = Mesh(mesh.devices.reshape(8, 2, 4, 4, 2), ("y", "zh", "x", "zl", "core"))
    in_specs = (
        P(BINS, None),
        P(BINS, None),
        P(VIEW, None),
        P(VIEW),
        P(None, BINS),
        P(),
        P(BINS),
        P(),
    )
    return jax.shard_map(
        local, mesh=fine, in_specs=in_specs, out_specs=P(BINS, None), check_vma=False
    )
```

```python
import jax
import jax.numpy as jnp
from jax import lax
from jax.experimental import pallas as pl
from jax.experimental.pallas import tpu as pltpu
from jax.sharding import Mesh, PartitionSpec as P

ROWS, HALF, K, CHUNKS, STEPS = 1024, 512, 128, 8, 128
PEERS, NVIEW, TRACKS = 64, 8, 640
BLOCK = 256
FINE = 64
TINY = 16
PART = STEPS + 8
BINS, VIEW = ("y", "zh", "x"), ("zl", "core")
VMEM, SMEM, HBM = pltpu.VMEM, pltpu.SMEM, pltpu.HBM
F32, BF16 = jnp.float32, jnp.bfloat16


def spec(space):
    return pl.BlockSpec(memory_space=space)


def call(body, ins, outs, scratch=()):
    return pl.pallas_call(
        body,
        in_specs=[spec(s) for s in ins],
        out_specs=[spec(VMEM) for _ in outs],
        out_shape=[jax.ShapeDtypeStruct(shape, dtype) for shape, dtype in outs],
        scratch_shapes=list(scratch),
        compiler_params=pltpu.CompilerParams(vmem_limit_bytes=48 * 1024 * 1024),
    )


def gains(span):
    forget = 1.0 / span
    return 1.0 - forget, jnp.sqrt(forget * (2.0 - forget))


def masked(carry, first, begin_ref):
    n = carry.shape[1]
    at = (
        first
        + lax.broadcasted_iota(jnp.int32, carry.shape, 0) * n
        + lax.broadcasted_iota(jnp.int32, carry.shape, 1)
    )
    begins = (at == begin_ref[0]) | (at == begin_ref[1]) | (at == begin_ref[2])
    return jnp.where(begins, 0.0, carry)


def column(carry, i):
    return jnp.broadcast_to(carry[:, i : i + 1], (CHUNKS, K))


def rows(ref, i, stride):
    return ref[pl.ds(i, CHUNKS, stride=stride), :]


def ends_kernel(
    here, begin_hbm, span_hbm, carry_hbm, x_hbm, d_hbm, chunk, sent,
    begin, span, carry_ref, x, d, xs, ds, sems,
):
    pairs = [(x_hbm, x), (d_hbm, d), (carry_hbm, carry_ref), (span_hbm, span), (begin_hbm, begin)]
    copies = [pltpu.make_async_copy(a, b, sems.at[i]) for i, (a, b) in enumerate(pairs)]
    for copy in copies:
        copy.start()
    for copy in copies[::-1]:
        copy.wait()
    keep, gain = gains(span[...])
    carry = masked(carry_ref[...], here[0] * ROWS, begin)
    xs[...] = gain * x[...].astype(F32)
    ds[...] = gain * d[...].astype(F32)
    half = STEPS // 2
    ends = []
    for first in (0, half):
        z, v = rows(xs, first, STEPS), rows(ds, first, STEPS)
        m = column(carry, first) * keep
        for i in range(first + 1, first + half):
            decay = column(carry, i) * keep
            z = decay * z + rows(xs, i, STEPS)
            v = decay * v + rows(ds, i, STEPS)
            m = decay * m
        ends.append((m, z, v))
    (m0, z0, v0), (m1, z1, v1) = ends
    m, z, v = m0 * m1, m1 * z0 + z1, m1 * v0 + v1
    chunk[0] = m
    chunk[1] = z
    chunk[2] = v
    mt, zt, vt = m[0:1], z[0:1], v[0:1]
    for j in range(1, CHUNKS):
        mj = m[j : j + 1]
        mt, zt, vt = mj * mt, mj * zt + z[j : j + 1], mj * vt + v[j : j + 1]
    sent[...] = jnp.broadcast_to(jnp.concatenate([mt, zt, vt], axis=0)[None], sent.shape)


def widen_kernel(chunk, coupling, assay, out):
    del chunk
    out[0:TRACKS, :] = coupling[...].astype(F32)
    lanes = [assay[:, i * K : (i + 1) * K] for i in range(TRACKS // K)]
    rest = jnp.zeros((8 - len(lanes), K), jnp.int32)
    out[TRACKS : TRACKS + 8, :] = jnp.concatenate(lanes + [rest], axis=0).astype(F32)


def prepare_kernel(
    here, begin, span, carry_wide, carry_fine, x, d, chunk, shift,
    latent, moved, product, shift_t, suffix, own_decay, xs, ds, decays,
):
    core, owned = here[2], here[2] * 4 + here[1]
    keep, gain = gains(span[...])
    start = pl.multiple_of(core * HALF, HALF)
    carry = masked(
        carry_fine[pl.ds(pl.multiple_of(core * CHUNKS, CHUNKS), CHUNKS), :],
        here[0] * ROWS + core * HALF,
        begin,
    )
    xs[...] = gain * x[pl.ds(start, HALF), :].astype(F32)
    ds[...] = gain * d[pl.ds(start, HALF), :].astype(F32)
    z, v = rows(xs, 0, FINE), rows(ds, 0, FINE)
    m = column(carry, 0) * keep
    for i in range(1, FINE):
        decay = column(carry, i) * keep
        z = decay * z + rows(xs, i, FINE)
        v = decay * v + rows(ds, i, FINE)
        m = decay * m
    q, ez, ev = jnp.ones((1, K), F32), jnp.zeros((1, K), F32), jnp.zeros((1, K), F32)
    for j in range(CHUNKS // 2):
        mj = chunk[0, j : j + 1, :]
        q, ez, ev = mj * q, mj * ez + chunk[1, j : j + 1, :], mj * ev + chunk[2, j : j + 1, :]
    second = core == 1
    qs, zs, vs = [jnp.where(second, q, 1.0)], [jnp.where(second, ez, 0.0)], [jnp.where(second, ev, 0.0)]
    for j in range(CHUNKS - 1):
        mj = m[j : j + 1]
        qs.append(mj * qs[-1])
        zs.append(mj * zs[-1] + z[j : j + 1])
        vs.append(mj * vs[-1] + v[j : j + 1])
    q, z, v = (jnp.concatenate(a, axis=0) for a in (qs, zs, vs))
    for i in range(FINE):
        decay = column(carry, i) * keep
        q = decay * q
        z = decay * z + rows(xs, i, FINE)
        v = decay * v + rows(ds, i, FINE)
        at = pl.ds(i, CHUNKS, stride=FINE)
        product[at, :] = q
        latent[at, :] = z
        moved[at, :] = v
    carry = masked(carry_wide[...], here[0] * ROWS, begin)
    f = jnp.ones((CHUNKS, K), F32)
    for i in reversed(range(STEPS)):
        decay = column(carry, i) * keep
        at = pl.ds(i, CHUNKS, stride=STEPS)
        suffix[at, :] = f
        decays[at, :] = decay
        f = decay * f
    own_decay[...] = decays[pl.ds(pl.multiple_of(owned * STEPS, STEPS), STEPS), :]
    s = shift[:, pl.ds(start, HALF)]
    hi = s.astype(BF16).astype(F32)
    mid = (s - hi).astype(BF16).astype(F32)
    low = s - hi - mid
    blank = jnp.zeros((K - 3 * NVIEW, HALF), F32)
    shift_t[...] = jnp.concatenate([hi, mid, low, blank], axis=0).T.astype(BF16)


def couple_kernel(mine, other, coupling_t, coupling):
    for side, ref in enumerate((mine, other)):
        at = pl.ds(side * TRACKS, TRACKS)
        w = ref[0:TRACKS, :]
        coupling[at, :] = w.astype(BF16)
        coupling_t[0:K, at] = w.T.astype(BF16)
        assay = ref[TRACKS : TRACKS + 8, :]
        assay = jnp.concatenate([assay[i : i + 1] for i in range(TRACKS // K)], axis=1)
        view = lax.broadcasted_iota(jnp.int32, (NVIEW, TRACKS), 0).astype(F32)
        member = (assay == view).astype(F32)
        blank = jnp.zeros((K - 3 * NVIEW, TRACKS), F32)
        coupling_t[K : 2 * K, at] = jnp.concatenate([member] * 3 + [blank], axis=0).astype(BF16)


def tracks_kernel(
    here, got, latent_ref, moved_ref, product_ref, shift_t, coupling_t, coupling,
    keep, send1, send2, send3, sent, pulled,
):
    ez = jnp.zeros((1, K), F32)
    ev = jnp.zeros((1, K), F32)
    for e in range(PEERS - 1):
        m, z, v = got[e, 0:1, :], got[e, 1:2, :], got[e, 2:3, :]
        earlier = e < here[0]
        ez = jnp.where(earlier, m * ez + z, ez)
        ev = jnp.where(earlier, m * ev + v, ev)
    total = jnp.zeros((1, K), F32)
    for b in range(HALF // BLOCK):
        at = pl.ds(b * BLOCK, BLOCK)
        product = product_ref[at, :]
        latent = (latent_ref[at, :] + product * ez).astype(BF16)
        moved = (moved_ref[at, :] + product * ev).astype(BF16)
        log_rate = jnp.dot(
            jnp.concatenate([latent, shift_t[at, :]], axis=1),
            coupling_t[...],
            preferred_element_type=F32,
        )
        along = jnp.dot(moved, coupling_t[0:K, :], preferred_element_type=F32)
        weighted = (jnp.exp(log_rate) * along).astype(BF16)
        p = jnp.dot(weighted, coupling[...], preferred_element_type=F32)
        pulled[at, :] = p
        total = total + jnp.sum(product * p, axis=0, keepdims=True)
    sent[...] = jnp.broadcast_to(total[None], sent.shape)
    for k, out in enumerate((keep, send1, send2, send3)):
        part = lax.rem(here[1] + k, 4)
        out[...] = pulled[pl.ds(pl.multiple_of(part * STEPS, STEPS), STEPS), :]


def weights_kernel(here, got, weights):
    w = jnp.ones((1, K), F32)
    for e in range(PEERS):
        later = e > here[0]
        weights[e] = jnp.where(later, w, 0.0)
        w = jnp.where(later, w * got[e, 0:1, :], w)


def sum_kernel(weights, late, own_decay, keep, got1, got2, got3, out, p, a):
    p[...] = (keep[...] + got1[...]) + (got2[...] + got3[...])
    r = jnp.zeros((CHUNKS, K), F32)
    m = jnp.ones((CHUNKS, K), F32)
    for i in reversed(range(TINY)):
        decay = rows(own_decay, i, TINY)
        r = decay * (rows(p, i, TINY) + r)
        m = decay * m
    entries = [jnp.zeros((1, K), F32)]
    for j in reversed(range(CHUNKS)):
        entries.append(m[j : j + 1] * entries[-1] + r[j : j + 1])
    total = entries.pop()
    r = jnp.concatenate(entries[::-1], axis=0)
    for i in reversed(range(TINY)):
        adjoint = rows(p, i, TINY) + r
        a[pl.ds(i, CHUNKS, stride=TINY), :] = adjoint
        r = rows(own_decay, i, TINY) * adjoint
    entry = jnp.sum(weights[...] * late[...], axis=0)
    tail = jnp.concatenate([total, entry, jnp.zeros((PART - STEPS - 2, K), F32)], axis=0)
    for j in range(4):
        out[j, 0:STEPS, :] = a[...]
        out[j, STEPS:PART, :] = tail


def finish_kernel(span, d, chunk, suffix, parts, out):
    _, gain = gains(span[...])
    entry = parts[0, STEPS + 1 : STEPS + 2, :]
    for j in range(1, CHUNKS):
        entry = entry + parts[j, STEPS + 1 : STEPS + 2, :]
    for j in reversed(range(CHUNKS)):
        at = pl.ds(j * STEPS, STEPS)
        adjoint = parts[j, 0:STEPS, :] + suffix[at, :] * entry
        out[at, :] = gain * adjoint + d[at, :].astype(F32)
        entry = chunk[0, j : j + 1, :] * entry + parts[j, STEPS : STEPS + 1, :]


def local(x, d, coupling, assay, shift, span, carry, begin):
    here = jnp.stack([lax.axis_index(BINS), lax.axis_index("zl"), lax.axis_index("core")])
    span = span.reshape(1, K)
    carry_wide = carry.reshape(CHUNKS, STEPS)
    wide = ((ROWS, K), F32)
    half = ((HALF, K), F32)
    tile = ((STEPS, K), F32)
    chunk, sent = call(
        ends_kernel,
        [SMEM] + [HBM] * 5,
        [((3, CHUNKS, K), F32), ((PEERS, 3, K), F32)],
        [
            SMEM((3,), jnp.int32),
            VMEM((1, K), F32),
            VMEM((CHUNKS, STEPS), F32),
            VMEM((ROWS, K), BF16),
            VMEM((ROWS, K), BF16),
            VMEM(*wide),
            VMEM(*wide),
            pltpu.SemaphoreType.DMA((5,)),
        ],
    )(here, begin, span, carry_wide, x, d)
    got = lax.all_to_all(sent, BINS, 0, 0, tiled=True)

    (mine,) = call(widen_kernel, [VMEM] * 3, [((TRACKS + 8, K), F32)])(
        chunk, coupling, assay.reshape(1, TRACKS)
    )
    other = lax.ppermute(mine, "core", [(0, 1), (1, 0)])
    latent, moved, product, shift_t, suffix, own_decay = call(
        prepare_kernel,
        [SMEM] * 2 + [VMEM] * 7,
        [half, half, half, ((HALF, K), BF16), wide, tile],
        [VMEM(*half), VMEM(*half), VMEM(*wide)],
    )(here, begin, span, carry_wide, carry.reshape(2 * CHUNKS, FINE), x, d, chunk, shift)
    coupling_t, both = call(
        couple_kernel, [VMEM] * 2, [((2 * K, 2 * TRACKS), BF16), ((2 * TRACKS, K), BF16)]
    )(mine, other)

    keep, send1, send2, send3, sent = call(
        tracks_kernel,
        [SMEM] + [VMEM] * 7,
        [tile] * 4 + [((PEERS, 1, K), F32)],
        [VMEM(*half)],
    )(here, got, latent, moved, product, shift_t, coupling_t, both)
    late = lax.all_to_all(sent, BINS, 0, 0, tiled=True)
    received = [
        lax.ppermute(s, "zl", [(i, (i + k) % 4) for i in range(4)])
        for k, s in ((1, send1), (2, send2), (3, send3))
    ]
    (weights,) = call(weights_kernel, [SMEM, VMEM], [((PEERS, 1, K), F32)])(here, got)
    (mine,) = call(
        sum_kernel, [VMEM] * 7, [((4, PART, K), F32)], [VMEM(*tile)] * 2
    )(weights, late, own_decay, keep, *received)
    quarter = lax.all_to_all(mine, "zl", 0, 0, tiled=True)
    parts = lax.all_gather(quarter, "core").reshape(CHUNKS, PART, K)
    (out,) = call(finish_kernel, [VMEM] * 5, [wide])(span, d, chunk, suffix, parts)
    return out


def solution(mesh):
    fine = Mesh(mesh.devices.reshape(8, 2, 4, 4, 2), ("y", "zh", "x", "zl", "core"))
    in_specs = (
        P(BINS, None),
        P(BINS, None),
        P(VIEW, None),
        P(VIEW),
        P(None, BINS),
        P(),
        P(BINS),
        P(),
    )
    return jax.shard_map(
        local, mesh=fine, in_specs=in_specs, out_specs=P(BINS, None), check_vma=False
    )
```

```python
import jax
import jax.numpy as jnp
from jax import lax
from jax.experimental import pallas as pl
from jax.experimental.pallas import tpu as pltpu
from jax.sharding import Mesh, PartitionSpec as P

ROWS, QUARTER, K, CHUNKS, STEPS = 1024, 256, 128, 8, 128
PEERS, NVIEW, TRACKS = 64, 8, 640
SHARD = TRACKS + 8
FINE = 32
TINY = 16
PART = STEPS + 8
BINS, VIEW = ("y", "zh", "x"), ("zl", "core")
VMEM, SMEM, HBM = pltpu.VMEM, pltpu.SMEM, pltpu.HBM
F32, BF16 = jnp.float32, jnp.bfloat16


def spec(space):
    return pl.BlockSpec(memory_space=space)


def call(body, ins, outs, scratch=(), vmem=16):
    return pl.pallas_call(
        body,
        in_specs=[spec(s) for s in ins],
        out_specs=[spec(VMEM) for _ in outs],
        out_shape=[jax.ShapeDtypeStruct(shape, dtype) for shape, dtype in outs],
        scratch_shapes=list(scratch),
        compiler_params=pltpu.CompilerParams(vmem_limit_bytes=vmem * 1024 * 1024),
    )


def gains(span):
    forget = 1.0 / span
    return 1.0 - forget, jnp.sqrt(forget * (2.0 - forget))


def masked(carry, first, begin_ref):
    m = carry.shape[1]
    at = (
        first
        + lax.broadcasted_iota(jnp.int32, carry.shape, 0) * m
        + lax.broadcasted_iota(jnp.int32, carry.shape, 1)
    )
    begins = (at == begin_ref[0]) | (at == begin_ref[1]) | (at == begin_ref[2])
    return jnp.where(begins, 0.0, carry)


def column(carry, i):
    return jnp.broadcast_to(carry[:, i : i + 1], (CHUNKS, K))


def rows(ref, i, stride):
    return ref[pl.ds(i, CHUNKS, stride=stride), :]


def ends_kernel(
    here, begin_hbm, span_hbm, carry_hbm, assay_hbm, coupling_hbm, x_hbm, d_hbm, chunk, sent, shard,
    begin, span, carry_ref, assay, coupling, x, d, xs, ds, sems,
):
    pairs = [
        (x_hbm, x),
        (d_hbm, d),
        (coupling_hbm, coupling),
        (assay_hbm, assay),
        (carry_hbm, carry_ref),
        (span_hbm, span),
        (begin_hbm, begin),
    ]
    copies = [pltpu.make_async_copy(a, b, sems.at[i]) for i, (a, b) in enumerate(pairs)]
    for copy in copies:
        copy.start()
    for copy in copies[::-1]:
        copy.wait()
    rest = jnp.zeros((SHARD - TRACKS - TRACKS // K, K), jnp.int32)
    shard[0:TRACKS, :] = coupling[...].astype(F32)
    shard[TRACKS:SHARD, :] = jnp.concatenate([assay[...], rest], axis=0).astype(F32)
    keep, gain = gains(span[...])
    carry = masked(carry_ref[...], here[0] * ROWS, begin)
    xs[...] = gain * x[...].astype(F32)
    ds[...] = gain * d[...].astype(F32)
    half = STEPS // 2
    ends = []
    for first in (0, half):
        z, v = rows(xs, first, STEPS), rows(ds, first, STEPS)
        m = column(carry, first) * keep
        for i in range(first + 1, first + half):
            decay = column(carry, i) * keep
            z = decay * z + rows(xs, i, STEPS)
            v = decay * v + rows(ds, i, STEPS)
            m = decay * m
        ends.append((m, z, v))
    (m0, z0, v0), (m1, z1, v1) = ends
    m, z, v = m0 * m1, m1 * z0 + z1, m1 * v0 + v1
    chunk[0] = m
    chunk[1] = z
    chunk[2] = v
    mt, zt, vt = m[0:1], z[0:1], v[0:1]
    for j in range(1, CHUNKS):
        mj = m[j : j + 1]
        mt, zt, vt = mj * mt, mj * zt + z[j : j + 1], mj * vt + v[j : j + 1]
    sent[...] = jnp.broadcast_to(jnp.concatenate([mt, zt, vt], axis=0)[None], sent.shape)


def prepare_kernel(
    here, zl, core, begin, span, carry_ref, x, d, chunk, shift,
    latent, moved, product, shift_t, xs, ds,
):
    at = core[0] * 4 + lax.rem(zl[0], 2) * 2
    start = pl.multiple_of(at * STEPS, QUARTER)
    keep, gain = gains(span[...])
    pair = masked(carry_ref[pl.ds(at, 2), :], here[0] * ROWS + start, begin)
    carry = jnp.concatenate(
        [pair[j : j + 1, i : i + FINE] for j in range(2) for i in range(0, STEPS, FINE)], axis=0
    )
    xs[...] = gain * x[pl.ds(start, QUARTER), :].astype(F32)
    ds[...] = gain * d[pl.ds(start, QUARTER), :].astype(F32)
    z, v = rows(xs, 0, FINE), rows(ds, 0, FINE)
    m = column(carry, 0) * keep
    for i in range(1, FINE):
        decay = column(carry, i) * keep
        z = decay * z + rows(xs, i, FINE)
        v = decay * v + rows(ds, i, FINE)
        m = decay * m
    q, ez, ev = jnp.ones((1, K), F32), jnp.zeros((1, K), F32), jnp.zeros((1, K), F32)
    for j in range(CHUNKS - 2):
        before = j < at
        mj, zj, vj = (chunk[i, j : j + 1, :] for i in range(3))
        q = jnp.where(before, mj * q, q)
        ez = jnp.where(before, mj * ez + zj, ez)
        ev = jnp.where(before, mj * ev + vj, ev)
    qs, zs, vs = [q], [ez], [ev]
    for j in range(CHUNKS - 1):
        mj = m[j : j + 1]
        qs.append(mj * qs[-1])
        zs.append(mj * zs[-1] + z[j : j + 1])
        vs.append(mj * vs[-1] + v[j : j + 1])
    q, z, v = (jnp.concatenate(a, axis=0) for a in (qs, zs, vs))
    for i in range(FINE):
        decay = column(carry, i) * keep
        q = decay * q
        z = decay * z + rows(xs, i, FINE)
        v = decay * v + rows(ds, i, FINE)
        to = pl.ds(i, CHUNKS, stride=FINE)
        product[to, :] = q
        latent[to, :] = z
        moved[to, :] = v
    s = shift[:, pl.ds(start, QUARTER)]
    hi = s.astype(BF16).astype(F32)
    mid = (s - hi).astype(BF16).astype(F32)
    low = s - hi - mid
    blank = jnp.zeros((K - 3 * NVIEW, QUARTER), F32)
    shift_t[...] = jnp.concatenate([hi, mid, low, blank], axis=0).T.astype(BF16)


def couple_kernel(mine, other, both):
    for side in range(4):
        ref = (mine, other)[side // 2].at[side % 2]
        at = pl.ds(side * TRACKS, TRACKS)
        w = ref[0:TRACKS, :]
        both[0:K, at] = w.T.astype(BF16)
        both[2 * K : 3 * K, at] = jnp.concatenate(
            [w[i : i + K] for i in range(0, TRACKS, K)], axis=1
        ).astype(BF16)
        assay = ref[TRACKS:SHARD, :]
        assay = jnp.concatenate([assay[i : i + 1] for i in range(TRACKS // K)], axis=1)
        view = lax.broadcasted_iota(jnp.int32, (NVIEW, TRACKS), 0).astype(F32)
        member = (assay == view).astype(F32)
        blank = jnp.zeros((K - 3 * NVIEW, TRACKS), F32)
        both[K : 2 * K, at] = jnp.concatenate([member] * 3 + [blank], axis=0).astype(BF16)


def tracks_kernel(
    here, zl, got, latent_ref, moved_ref, product_ref, shift_t, both,
    keep, send, sent, pulled,
):
    ez = jnp.zeros((1, K), F32)
    ev = jnp.zeros((1, K), F32)
    for e in range(PEERS - 1):
        m, z, v = got[e, 0:1, :], got[e, 1:2, :], got[e, 2:3, :]
        earlier = e < here[0]
        ez = jnp.where(earlier, m * ez + z, ez)
        ev = jnp.where(earlier, m * ev + v, ev)
    product = product_ref[...]
    latent = (latent_ref[...] + product * ez).astype(BF16)
    latent = jnp.concatenate([latent, shift_t[...]], axis=1)
    moved = (moved_ref[...] + product * ev).astype(BF16)
    p = jnp.zeros((QUARTER, K), F32)
    for side in range(4):
        at = pl.ds(side * TRACKS, TRACKS)
        log_rate = jnp.dot(latent, both[0 : 2 * K, at], preferred_element_type=F32)
        along = jnp.dot(moved, both[0:K, at], preferred_element_type=F32)
        weighted = (jnp.exp(log_rate) * along).astype(BF16)
        blocks = both[2 * K : 3 * K, at]
        coupling = jnp.concatenate([blocks[:, i : i + K] for i in range(0, TRACKS, K)], axis=0)
        p = p + jnp.dot(weighted, coupling, preferred_element_type=F32)
    pulled[...] = p
    total = jnp.sum(product * p, axis=0, keepdims=True)
    sent[...] = jnp.broadcast_to(total[None], sent.shape)
    own = lax.div(zl[0], 2)
    keep[...] = pulled[pl.ds(pl.multiple_of(own * STEPS, STEPS), STEPS), :]
    send[...] = pulled[pl.ds(pl.multiple_of((1 - own) * STEPS, STEPS), STEPS), :]


def later_kernel(here, zl, core, begin, span, carry_ref, got, weights, suffix, own_decay, decays):
    w = jnp.ones((1, K), F32)
    for e in range(PEERS):
        later = e > here[0]
        weights[e] = jnp.where(later, w, 0.0)
        w = jnp.where(later, w * got[e, 0:1, :], w)
    keep, _ = gains(span[...])
    carry = masked(carry_ref[...], here[0] * ROWS, begin)
    f = jnp.ones((CHUNKS, K), F32)
    for i in reversed(range(STEPS)):
        decay = column(carry, i) * keep
        to = pl.ds(i, CHUNKS, stride=STEPS)
        suffix[to, :] = f
        decays[to, :] = decay
        f = decay * f
    owned = core[0] * 4 + lax.rem(zl[0], 2) * 2 + lax.div(zl[0], 2)
    owned = pl.multiple_of(owned * STEPS, STEPS)
    own_decay[...] = decays[pl.ds(owned, STEPS), :]


def sum_kernel(weights, late, own_decay, keep, got, out, p, a):
    p[...] = keep[...] + got[...]
    r = jnp.zeros((CHUNKS, K), F32)
    m = jnp.ones((CHUNKS, K), F32)
    for i in reversed(range(TINY)):
        decay = rows(own_decay, i, TINY)
        r = decay * (rows(p, i, TINY) + r)
        m = decay * m
    entries = [jnp.zeros((1, K), F32)]
    for j in reversed(range(CHUNKS)):
        entries.append(m[j : j + 1] * entries[-1] + r[j : j + 1])
    total = entries.pop()
    r = jnp.concatenate(entries[::-1], axis=0)
    for i in reversed(range(TINY)):
        adjoint = rows(p, i, TINY) + r
        a[pl.ds(i, CHUNKS, stride=TINY), :] = adjoint
        r = rows(own_decay, i, TINY) * adjoint
    entry = jnp.sum(weights[...] * late[...], axis=0)
    tail = jnp.concatenate([total, entry, jnp.zeros((PART - STEPS - 2, K), F32)], axis=0)
    for j in range(4):
        out[j, 0:STEPS, :] = a[...]
        out[j, STEPS:PART, :] = tail


def finish_kernel(span, d, chunk, suffix, parts, out):
    _, gain = gains(span[...])
    entry = parts[0, STEPS + 1 : STEPS + 2, :]
    for j in range(1, CHUNKS):
        entry = entry + parts[j, STEPS + 1 : STEPS + 2, :]
    for j in reversed(range(CHUNKS)):
        at = pl.ds(j * STEPS, STEPS)
        part = j // 4 * 4 + j % 2 * 2 + j // 2 % 2
        adjoint = parts[part, 0:STEPS, :] + suffix[at, :] * entry
        out[at, :] = gain * adjoint + d[at, :].astype(F32)
        entry = chunk[0, j : j + 1, :] * entry + parts[part, STEPS : STEPS + 1, :]


def local(x, d, coupling, assay, shift, span, carry, begin):
    here = lax.axis_index(BINS)[None]
    zl, core = lax.axis_index("zl")[None], lax.axis_index("core")[None]
    span = span.reshape(1, K)
    carry = carry.reshape(CHUNKS, STEPS)
    wide, quarter, tile = ((ROWS, K), F32), ((QUARTER, K), F32), ((STEPS, K), F32)
    chunk, sent, shard = call(
        ends_kernel,
        [SMEM] + [HBM] * 7,
        [((3, CHUNKS, K), F32), ((PEERS, 3, K), F32), ((SHARD, K), F32)],
        [
            SMEM((3,), jnp.int32),
            VMEM((1, K), F32),
            VMEM((CHUNKS, STEPS), F32),
            VMEM((TRACKS // K, K), jnp.int32),
            VMEM((TRACKS, K), BF16),
            VMEM((ROWS, K), BF16),
            VMEM((ROWS, K), BF16),
            VMEM(*wide),
            VMEM(*wide),
            pltpu.SemaphoreType.DMA((7,)),
        ],
        vmem=60,
    )(here, begin, span, carry, assay.reshape(TRACKS // K, K), coupling, x, d)
    got = lax.all_to_all(sent, BINS, 0, 0, tiled=True)

    mine = lax.all_gather(shard, "core")
    other = lax.ppermute(mine, "zl", [(i, i ^ 1) for i in range(4)])
    (both,) = call(couple_kernel, [VMEM] * 2, [((3 * K, 4 * TRACKS), BF16)])(mine, other)
    latent, moved, product, shift_t = call(
        prepare_kernel,
        [SMEM] * 4 + [VMEM] * 6,
        [quarter, quarter, quarter, ((QUARTER, K), BF16)],
        [VMEM(*quarter), VMEM(*quarter)],
    )(here, zl, core, begin, span, carry, x, d, chunk, shift)

    keep, send, sent = call(
        tracks_kernel,
        [SMEM] * 2 + [VMEM] * 6,
        [tile] * 2 + [((PEERS, 1, K), F32)],
        [VMEM(*quarter)],
    )(here, zl, got, latent, moved, product, shift_t, both)
    late = lax.all_to_all(sent, BINS, 0, 0, tiled=True)
    received = lax.ppermute(send, "zl", [(i, i ^ 2) for i in range(4)])
    weights, suffix, own_decay = call(
        later_kernel,
        [SMEM] * 4 + [VMEM] * 3,
        [((PEERS, 1, K), F32), wide, tile],
        [VMEM(*wide)],
    )(here, zl, core, begin, span, carry, got)
    (mine,) = call(sum_kernel, [VMEM] * 5, [((4, PART, K), F32)], [VMEM(*tile)] * 2)(
        weights, late, own_decay, keep, received
    )
    column_parts = lax.all_to_all(mine, "zl", 0, 0, tiled=True)
    parts = lax.all_gather(column_parts, "core").reshape(CHUNKS, PART, K)
    (out,) = call(finish_kernel, [VMEM] * 5, [wide])(span, d, chunk, suffix, parts)
    return out


def solution(mesh):
    fine = Mesh(mesh.devices.reshape(8, 2, 4, 4, 2), ("y", "zh", "x", "zl", "core"))
    in_specs = (
        P(BINS, None),
        P(BINS, None),
        P(VIEW, None),
        P(VIEW),
        P(None, BINS),
        P(),
        P(BINS),
        P(),
    )
    return jax.shard_map(
        local, mesh=fine, in_specs=in_specs, out_specs=P(BINS, None), check_vma=False
    )
```

```python
import jax
import jax.numpy as jnp
from jax import lax
from jax.experimental import pallas as pl
from jax.experimental.pallas import tpu as pltpu
from jax.sharding import Mesh, PartitionSpec as P

ROWS, QUARTER, K, CHUNKS, STEPS = 1024, 256, 128, 8, 128
PEERS, NVIEW, TRACKS = 64, 8, 640
SHARD = TRACKS + 8
FINE = 32
TINY = 16
PART = STEPS + 8
BINS, VIEW = ("y", "zh", "x"), ("zl", "core")
VMEM, SMEM, HBM = pltpu.VMEM, pltpu.SMEM, pltpu.HBM
F32, BF16 = jnp.float32, jnp.bfloat16


def spec(space):
    return pl.BlockSpec(memory_space=space)


def call(body, ins, outs, scratch=(), vmem=16):
    return pl.pallas_call(
        body,
        in_specs=[spec(s) for s in ins],
        out_specs=[spec(VMEM) for _ in outs],
        out_shape=[jax.ShapeDtypeStruct(shape, dtype) for shape, dtype in outs],
        scratch_shapes=list(scratch),
        compiler_params=pltpu.CompilerParams(vmem_limit_bytes=vmem * 1024 * 1024),
    )


def gains(span):
    forget = 1.0 / span
    return 1.0 - forget, jnp.sqrt(forget * (2.0 - forget))


def masked(carry, first, begin_ref):
    m = carry.shape[1]
    at = (
        first
        + lax.broadcasted_iota(jnp.int32, carry.shape, 0) * m
        + lax.broadcasted_iota(jnp.int32, carry.shape, 1)
    )
    begins = (at == begin_ref[0]) | (at == begin_ref[1]) | (at == begin_ref[2])
    return jnp.where(begins, 0.0, carry)


def column(carry, i):
    return jnp.broadcast_to(carry[:, i : i + 1], (CHUNKS, K))


def rows(ref, i, stride):
    return ref[pl.ds(i, CHUNKS, stride=stride), :]


def ends_kernel(
    here, begin_hbm, span_hbm, carry_hbm, assay_hbm, coupling_hbm, x_hbm, d_hbm, chunk, sent, shard,
    begin, span, carry_ref, assay, coupling, x, d, xs, ds, sems,
):
    pairs = [
        (x_hbm, x),
        (d_hbm, d),
        (coupling_hbm, coupling),
        (assay_hbm, assay),
        (carry_hbm, carry_ref),
        (span_hbm, span),
        (begin_hbm, begin),
    ]
    copies = [pltpu.make_async_copy(a, b, sems.at[i]) for i, (a, b) in enumerate(pairs)]
    for copy in copies:
        copy.start()
    for copy in copies[::-1]:
        copy.wait()
    rest = jnp.zeros((SHARD - TRACKS - TRACKS // K, K), jnp.int32)
    shard[0:TRACKS, :] = coupling[...].astype(F32)
    shard[TRACKS:SHARD, :] = jnp.concatenate([assay[...], rest], axis=0).astype(F32)
    keep, gain = gains(span[...])
    carry = masked(carry_ref[...], here[0] * ROWS, begin)
    xs[...] = gain * x[...].astype(F32)
    ds[...] = gain * d[...].astype(F32)
    half = STEPS // 2
    ends = []
    for first in (0, half):
        z, v = rows(xs, first, STEPS), rows(ds, first, STEPS)
        m = column(carry, first) * keep
        for i in range(first + 1, first + half):
            decay = column(carry, i) * keep
            z = decay * z + rows(xs, i, STEPS)
            v = decay * v + rows(ds, i, STEPS)
            m = decay * m
        ends.append((m, z, v))
    (m0, z0, v0), (m1, z1, v1) = ends
    m, z, v = m0 * m1, m1 * z0 + z1, m1 * v0 + v1
    chunk[0] = m
    chunk[1] = z
    chunk[2] = v
    mt, zt, vt = m[0:1], z[0:1], v[0:1]
    for j in range(1, CHUNKS):
        mj = m[j : j + 1]
        mt, zt, vt = mj * mt, mj * zt + z[j : j + 1], mj * vt + v[j : j + 1]
    sent[...] = jnp.broadcast_to(jnp.concatenate([mt, zt, vt], axis=0)[None], sent.shape)


def prepare_kernel(
    here, zl, core, begin, span, carry_ref, x, d, chunk, shift, mine,
    latent, moved, product, shift_t, both, xs, ds,
):
    at = core[0] * 4 + lax.rem(zl[0], 2) * 2
    start = pl.multiple_of(at * STEPS, QUARTER)
    keep, gain = gains(span[...])
    pair = masked(carry_ref[pl.ds(at, 2), :], here[0] * ROWS + start, begin)
    carry = jnp.concatenate(
        [pair[j : j + 1, i : i + FINE] for j in range(2) for i in range(0, STEPS, FINE)], axis=0
    )
    xs[...] = gain * x[pl.ds(start, QUARTER), :].astype(F32)
    ds[...] = gain * d[pl.ds(start, QUARTER), :].astype(F32)
    z, v = rows(xs, 0, FINE), rows(ds, 0, FINE)
    m = column(carry, 0) * keep
    for i in range(1, FINE):
        decay = column(carry, i) * keep
        z = decay * z + rows(xs, i, FINE)
        v = decay * v + rows(ds, i, FINE)
        m = decay * m
    q, ez, ev = jnp.ones((1, K), F32), jnp.zeros((1, K), F32), jnp.zeros((1, K), F32)
    for j in range(CHUNKS - 2):
        before = j < at
        mj, zj, vj = (chunk[i, j : j + 1, :] for i in range(3))
        q = jnp.where(before, mj * q, q)
        ez = jnp.where(before, mj * ez + zj, ez)
        ev = jnp.where(before, mj * ev + vj, ev)
    qs, zs, vs = [q], [ez], [ev]
    for j in range(CHUNKS - 1):
        mj = m[j : j + 1]
        qs.append(mj * qs[-1])
        zs.append(mj * zs[-1] + z[j : j + 1])
        vs.append(mj * vs[-1] + v[j : j + 1])
    q, z, v = (jnp.concatenate(a, axis=0) for a in (qs, zs, vs))
    for i in range(FINE):
        decay = column(carry, i) * keep
        q = decay * q
        z = decay * z + rows(xs, i, FINE)
        v = decay * v + rows(ds, i, FINE)
        to = pl.ds(i, CHUNKS, stride=FINE)
        product[to, :] = q
        latent[to, :] = z
        moved[to, :] = v
    s = shift[:, pl.ds(start, QUARTER)]
    hi = s.astype(BF16).astype(F32)
    mid = (s - hi).astype(BF16).astype(F32)
    low = s - hi - mid
    blank = jnp.zeros((K - 3 * NVIEW, QUARTER), F32)
    shift_t[...] = jnp.concatenate([hi, mid, low, blank], axis=0).T.astype(BF16)
    couple(mine, both)


def couple(shards, both):
    for side in range(2):
        ref = shards.at[side]
        at = pl.ds(side * TRACKS, TRACKS)
        w = ref[0:TRACKS, :]
        both[0:K, at] = w.T.astype(BF16)
        both[2 * K : 3 * K, at] = jnp.concatenate(
            [w[i : i + K] for i in range(0, TRACKS, K)], axis=1
        ).astype(BF16)
        assay = ref[TRACKS:SHARD, :]
        assay = jnp.concatenate([assay[i : i + 1] for i in range(TRACKS // K)], axis=1)
        view = lax.broadcasted_iota(jnp.int32, (NVIEW, TRACKS), 0).astype(F32)
        member = (assay == view).astype(F32)
        blank = jnp.zeros((K - 3 * NVIEW, TRACKS), F32)
        both[K : 2 * K, at] = jnp.concatenate([member] * 3 + [blank], axis=0).astype(BF16)


def tracks_kernel(
    here, zl, got, latent_ref, moved_ref, product_ref, shift_t, mine, other,
    keep, send, sent, pulled, theirs,
):
    couple(other, theirs)
    ez = jnp.zeros((1, K), F32)
    ev = jnp.zeros((1, K), F32)
    for e in range(PEERS - 1):
        m, z, v = got[e, 0:1, :], got[e, 1:2, :], got[e, 2:3, :]
        earlier = e < here[0]
        ez = jnp.where(earlier, m * ez + z, ez)
        ev = jnp.where(earlier, m * ev + v, ev)
    product = product_ref[...]
    latent = (latent_ref[...] + product * ez).astype(BF16)
    latent = jnp.concatenate([latent, shift_t[...]], axis=1)
    moved = (moved_ref[...] + product * ev).astype(BF16)
    p = jnp.zeros((QUARTER, K), F32)
    for side in range(4):
        both, at = (mine, theirs)[side // 2], pl.ds(side % 2 * TRACKS, TRACKS)
        log_rate = jnp.dot(latent, both[0 : 2 * K, at], preferred_element_type=F32)
        along = jnp.dot(moved, both[0:K, at], preferred_element_type=F32)
        weighted = (jnp.exp(log_rate) * along).astype(BF16)
        blocks = both[2 * K : 3 * K, at]
        coupling = jnp.concatenate([blocks[:, i : i + K] for i in range(0, TRACKS, K)], axis=0)
        p = p + jnp.dot(weighted, coupling, preferred_element_type=F32)
    pulled[...] = p
    total = jnp.sum(product * p, axis=0, keepdims=True)
    sent[...] = jnp.broadcast_to(total[None], sent.shape)
    own = lax.div(zl[0], 2)
    keep[...] = pulled[pl.ds(pl.multiple_of(own * STEPS, STEPS), STEPS), :]
    send[...] = pulled[pl.ds(pl.multiple_of((1 - own) * STEPS, STEPS), STEPS), :]


def later_kernel(here, zl, core, begin, span, carry_ref, got, weights, suffix, own_decay, decays):
    w = jnp.ones((1, K), F32)
    for e in range(PEERS):
        later = e > here[0]
        weights[e] = jnp.where(later, w, 0.0)
        w = jnp.where(later, w * got[e, 0:1, :], w)
    keep, _ = gains(span[...])
    carry = masked(carry_ref[...], here[0] * ROWS, begin)
    f = jnp.ones((CHUNKS, K), F32)
    for i in reversed(range(STEPS)):
        decay = column(carry, i) * keep
        to = pl.ds(i, CHUNKS, stride=STEPS)
        suffix[to, :] = f
        decays[to, :] = decay
        f = decay * f
    owned = core[0] * 4 + lax.rem(zl[0], 2) * 2 + lax.div(zl[0], 2)
    owned = pl.multiple_of(owned * STEPS, STEPS)
    own_decay[...] = decays[pl.ds(owned, STEPS), :]


def sum_kernel(weights, late, own_decay, keep, got, out, p, a):
    p[...] = keep[...] + got[...]
    r = jnp.zeros((CHUNKS, K), F32)
    m = jnp.ones((CHUNKS, K), F32)
    for i in reversed(range(TINY)):
        decay = rows(own_decay, i, TINY)
        r = decay * (rows(p, i, TINY) + r)
        m = decay * m
    entries = [jnp.zeros((1, K), F32)]
    for j in reversed(range(CHUNKS)):
        entries.append(m[j : j + 1] * entries[-1] + r[j : j + 1])
    total = entries.pop()
    r = jnp.concatenate(entries[::-1], axis=0)
    for i in reversed(range(TINY)):
        adjoint = rows(p, i, TINY) + r
        a[pl.ds(i, CHUNKS, stride=TINY), :] = adjoint
        r = rows(own_decay, i, TINY) * adjoint
    entry = jnp.sum(weights[...] * late[...], axis=0)
    tail = jnp.concatenate([total, entry, jnp.zeros((PART - STEPS - 2, K), F32)], axis=0)
    for j in range(4):
        out[j, 0:STEPS, :] = a[...]
        out[j, STEPS:PART, :] = tail


def finish_kernel(span, d, chunk, suffix, parts, out):
    _, gain = gains(span[...])
    entry = parts[0, STEPS + 1 : STEPS + 2, :]
    for j in range(1, CHUNKS):
        entry = entry + parts[j, STEPS + 1 : STEPS + 2, :]
    for j in reversed(range(CHUNKS)):
        at = pl.ds(j * STEPS, STEPS)
        part = j // 4 * 4 + j % 2 * 2 + j // 2 % 2
        adjoint = parts[part, 0:STEPS, :] + suffix[at, :] * entry
        out[at, :] = gain * adjoint + d[at, :].astype(F32)
        entry = chunk[0, j : j + 1, :] * entry + parts[part, STEPS : STEPS + 1, :]


def local(x, d, coupling, assay, shift, span, carry, begin):
    here = lax.axis_index(BINS)[None]
    zl, core = lax.axis_index("zl")[None], lax.axis_index("core")[None]
    span = span.reshape(1, K)
    carry = carry.reshape(CHUNKS, STEPS)
    wide, quarter, tile = ((ROWS, K), F32), ((QUARTER, K), F32), ((STEPS, K), F32)
    packed = ((3 * K, 2 * TRACKS), BF16)
    chunk, sent, shard = call(
        ends_kernel,
        [SMEM] + [HBM] * 7,
        [((3, CHUNKS, K), F32), ((PEERS, 3, K), F32), ((SHARD, K), F32)],
        [
            SMEM((3,), jnp.int32),
            VMEM((1, K), F32),
            VMEM((CHUNKS, STEPS), F32),
            VMEM((TRACKS // K, K), jnp.int32),
            VMEM((TRACKS, K), BF16),
            VMEM((ROWS, K), BF16),
            VMEM((ROWS, K), BF16),
            VMEM(*wide),
            VMEM(*wide),
            pltpu.SemaphoreType.DMA((7,)),
        ],
        vmem=60,
    )(here, begin, span, carry, assay.reshape(TRACKS // K, K), coupling, x, d)
    got = lax.all_to_all(sent, BINS, 0, 0, tiled=True)

    mine = lax.all_gather(shard, "core")
    other = lax.ppermute(mine, "zl", [(i, i ^ 1) for i in range(4)])
    latent, moved, product, shift_t, both = call(
        prepare_kernel,
        [SMEM] * 4 + [VMEM] * 7,
        [quarter, quarter, quarter, ((QUARTER, K), BF16), packed],
        [VMEM(*quarter), VMEM(*quarter)],
    )(here, zl, core, begin, span, carry, x, d, chunk, shift, mine)

    keep, send, sent = call(
        tracks_kernel,
        [SMEM] * 2 + [VMEM] * 7,
        [tile] * 2 + [((PEERS, 1, K), F32)],
        [VMEM(*quarter), VMEM(*packed)],
    )(here, zl, got, latent, moved, product, shift_t, both, other)
    late = lax.all_to_all(sent, BINS, 0, 0, tiled=True)
    received = lax.ppermute(send, "zl", [(i, i ^ 2) for i in range(4)])
    weights, suffix, own_decay = call(
        later_kernel,
        [SMEM] * 4 + [VMEM] * 3,
        [((PEERS, 1, K), F32), wide, tile],
        [VMEM(*wide)],
    )(here, zl, core, begin, span, carry, got)
    (mine,) = call(sum_kernel, [VMEM] * 5, [((4, PART, K), F32)], [VMEM(*tile)] * 2)(
        weights, late, own_decay, keep, received
    )
    column_parts = lax.all_to_all(mine, "zl", 0, 0, tiled=True)
    parts = lax.all_gather(column_parts, "core").reshape(CHUNKS, PART, K)
    (out,) = call(finish_kernel, [VMEM] * 5, [wide])(span, d, chunk, suffix, parts)
    return out


def solution(mesh):
    fine = Mesh(mesh.devices.reshape(8, 2, 4, 4, 2), ("y", "zh", "x", "zl", "core"))
    in_specs = (
        P(BINS, None),
        P(BINS, None),
        P(VIEW, None),
        P(VIEW),
        P(None, BINS),
        P(),
        P(BINS),
        P(),
    )
    return jax.shard_map(
        local, mesh=fine, in_specs=in_specs, out_specs=P(BINS, None), check_vma=False
    )
```

```python
import jax
import jax.numpy as jnp
from jax import lax
from jax.experimental import pallas as pl
from jax.experimental.pallas import tpu as pltpu
from jax.sharding import Mesh, PartitionSpec as P

ROWS, QUARTER, K, CHUNKS, STEPS = 1024, 256, 128, 8, 128
PEERS, NVIEW, TRACKS = 64, 8, 640
SHARD = TRACKS + 8
FINE = 32
PAD = STEPS + 8
PART = QUARTER + 8
BINS, VIEW = ("y", "zh", "x"), ("zb", "za", "core")
VMEM, SMEM, HBM = pltpu.VMEM, pltpu.SMEM, pltpu.HBM
F32, BF16 = jnp.float32, jnp.bfloat16


def spec(space):
    return pl.BlockSpec(memory_space=space)


def call(body, ins, outs, scratch=(), vmem=16, spaces=None):
    return pl.pallas_call(
        body,
        in_specs=[spec(s) for s in ins],
        out_specs=[spec(s) for s in spaces or [VMEM] * len(outs)],
        out_shape=[jax.ShapeDtypeStruct(shape, dtype) for shape, dtype in outs],
        scratch_shapes=list(scratch),
        compiler_params=pltpu.CompilerParams(vmem_limit_bytes=vmem * 1024 * 1024),
    )


def gains(span):
    forget = 1.0 / span
    return 1.0 - forget, jnp.sqrt(forget * (2.0 - forget))


def masked(carry, first, begin_ref):
    m = carry.shape[1]
    at = (
        first
        + lax.broadcasted_iota(jnp.int32, carry.shape, 0) * m
        + lax.broadcasted_iota(jnp.int32, carry.shape, 1)
    )
    begins = (at == begin_ref[0]) | (at == begin_ref[1]) | (at == begin_ref[2])
    return jnp.where(begins, 0.0, carry)


def column(carry, i):
    return jnp.broadcast_to(carry[:, i : i + 1], (CHUNKS, K))


def rows(ref, i, stride):
    return ref[pl.ds(i, CHUNKS, stride=stride), :]


def ends_kernel(
    here, begin_hbm, span_hbm, carry_hbm, assay_hbm, coupling_hbm, x_hbm, d_hbm,
    chunk, sent, shard_hbm,
    begin, span, carry_ref, assay, coupling, x, d, shard, xs, ds, sems,
):
    pairs = [
        (coupling_hbm, coupling),
        (assay_hbm, assay),
        (carry_hbm, carry_ref),
        (span_hbm, span),
        (begin_hbm, begin),
        (x_hbm, x),
        (d_hbm, d),
    ]
    copies = [pltpu.make_async_copy(a, b, sems.at[i]) for i, (a, b) in enumerate(pairs)]
    for copy in copies:
        copy.start()
    copies[0].wait()
    copies[1].wait()
    rest = jnp.zeros((SHARD - TRACKS - TRACKS // K, K), jnp.int32)
    shard[0:TRACKS, :] = coupling[...].astype(F32)
    shard[TRACKS:SHARD, :] = jnp.concatenate([assay[...], rest], axis=0).astype(F32)
    leave = pltpu.make_async_copy(shard, shard_hbm, sems.at[len(pairs)])
    leave.start()
    for copy in copies[2:]:
        copy.wait()
    keep, gain = gains(span[...])
    carry = masked(carry_ref[...], here[0] * ROWS, begin)
    for j in range(CHUNKS):
        at, to = pl.ds(j * STEPS, STEPS), pl.ds(j * PAD, STEPS)
        xs[to, :] = gain * x[at, :].astype(F32)
        ds[to, :] = gain * d[at, :].astype(F32)
    half = STEPS // 2
    ends = []
    for first in (0, half):
        z, v = rows(xs, first, PAD), rows(ds, first, PAD)
        m = column(carry, first) * keep
        for i in range(first + 1, first + half):
            decay = column(carry, i) * keep
            z = decay * z + rows(xs, i, PAD)
            v = decay * v + rows(ds, i, PAD)
            m = decay * m
        ends.append((m, z, v))
    (m0, z0, v0), (m1, z1, v1) = ends
    m, z, v = m0 * m1, m1 * z0 + z1, m1 * v0 + v1
    chunk[0] = m
    chunk[1] = z
    chunk[2] = v
    mt, zt, vt = m[0:1], z[0:1], v[0:1]
    for j in range(1, CHUNKS):
        mj = m[j : j + 1]
        mt, zt, vt = mj * mt, mj * zt + z[j : j + 1], mj * vt + v[j : j + 1]
    sent[...] = jnp.broadcast_to(jnp.concatenate([mt, zt, vt], axis=0)[None], sent.shape)
    leave.wait()


def prepare_kernel(
    here, za, core, begin, span, carry_ref, x, d, chunk, shift, mine,
    latent, moved, product, shift_t, both, xs, ds,
):
    at = core[0] * 4 + za[0] * 2
    start = pl.multiple_of(at * STEPS, QUARTER)
    keep, gain = gains(span[...])
    pair = masked(carry_ref[pl.ds(at, 2), :], here[0] * ROWS + start, begin)
    carry = jnp.concatenate(
        [pair[j : j + 1, i : i + FINE] for j in range(2) for i in range(0, STEPS, FINE)], axis=0
    )
    xs[...] = gain * x[pl.ds(start, QUARTER), :].astype(F32)
    ds[...] = gain * d[pl.ds(start, QUARTER), :].astype(F32)
    z, v = rows(xs, 0, FINE), rows(ds, 0, FINE)
    m = column(carry, 0) * keep
    for i in range(1, FINE):
        decay = column(carry, i) * keep
        z = decay * z + rows(xs, i, FINE)
        v = decay * v + rows(ds, i, FINE)
        m = decay * m
    q, ez, ev = jnp.ones((1, K), F32), jnp.zeros((1, K), F32), jnp.zeros((1, K), F32)
    for j in range(CHUNKS - 2):
        before = j < at
        mj, zj, vj = (chunk[i, j : j + 1, :] for i in range(3))
        q = jnp.where(before, mj * q, q)
        ez = jnp.where(before, mj * ez + zj, ez)
        ev = jnp.where(before, mj * ev + vj, ev)
    qs, zs, vs = [q], [ez], [ev]
    for j in range(CHUNKS - 1):
        mj = m[j : j + 1]
        qs.append(mj * qs[-1])
        zs.append(mj * zs[-1] + z[j : j + 1])
        vs.append(mj * vs[-1] + v[j : j + 1])
    q, z, v = (jnp.concatenate(a, axis=0) for a in (qs, zs, vs))
    for i in range(FINE):
        decay = column(carry, i) * keep
        q = decay * q
        z = decay * z + rows(xs, i, FINE)
        v = decay * v + rows(ds, i, FINE)
        to = pl.ds(i, CHUNKS, stride=FINE)
        product[to, :] = q
        latent[to, :] = z
        moved[to, :] = v
    s = shift[:, pl.ds(start, QUARTER)]
    hi = s.astype(BF16).astype(F32)
    mid = (s - hi).astype(BF16).astype(F32)
    low = s - hi - mid
    blank = jnp.zeros((K - 3 * NVIEW, QUARTER), F32)
    shift_t[...] = jnp.concatenate([hi, mid, low, blank], axis=0).T.astype(BF16)
    couple(mine, both)


def couple(shards, both):
    for side in range(2):
        ref = shards.at[side]
        at = pl.ds(side * TRACKS, TRACKS)
        w = ref[0:TRACKS, :]
        both[0:K, at] = w.T.astype(BF16)
        both[2 * K : 3 * K, at] = jnp.concatenate(
            [w[i : i + K] for i in range(0, TRACKS, K)], axis=1
        ).astype(BF16)
        assay = ref[TRACKS:SHARD, :]
        assay = jnp.concatenate([assay[i : i + 1] for i in range(TRACKS // K)], axis=1)
        view = lax.broadcasted_iota(jnp.int32, (NVIEW, TRACKS), 0).astype(F32)
        member = (assay == view).astype(F32)
        blank = jnp.zeros((K - 3 * NVIEW, TRACKS), F32)
        both[K : 2 * K, at] = jnp.concatenate([member] * 3 + [blank], axis=0).astype(BF16)


def tracks_kernel(
    here, got, latent_ref, moved_ref, product_ref, shift_t, mine, other,
    pulled, sent, theirs,
):
    couple(other, theirs)
    ez = jnp.zeros((1, K), F32)
    ev = jnp.zeros((1, K), F32)
    for e in range(PEERS - 1):
        m, z, v = got[e, 0:1, :], got[e, 1:2, :], got[e, 2:3, :]
        earlier = e < here[0]
        ez = jnp.where(earlier, m * ez + z, ez)
        ev = jnp.where(earlier, m * ev + v, ev)
    product = product_ref[...]
    latent = (latent_ref[...] + product * ez).astype(BF16)
    latent = jnp.concatenate([latent, shift_t[...]], axis=1)
    moved = (moved_ref[...] + product * ev).astype(BF16)
    p = jnp.zeros((QUARTER, K), F32)
    for side in range(4):
        both, at = (mine, theirs)[side // 2], pl.ds(side % 2 * TRACKS, TRACKS)
        log_rate = jnp.dot(latent, both[0 : 2 * K, at], preferred_element_type=F32)
        along = jnp.dot(moved, both[0:K, at], preferred_element_type=F32)
        weighted = (jnp.exp(log_rate) * along).astype(BF16)
        blocks = both[2 * K : 3 * K, at]
        coupling = jnp.concatenate([blocks[:, i : i + K] for i in range(0, TRACKS, K)], axis=0)
        p = p + jnp.dot(weighted, coupling, preferred_element_type=F32)
    pulled[...] = p
    total = jnp.sum(product * p, axis=0, keepdims=True)
    sent[...] = jnp.broadcast_to(total[None], sent.shape)


def later_kernel(here, za, core, begin, span, carry_ref, got, weights, suffix, own_decay, decays):
    w = jnp.ones((1, K), F32)
    for e in range(PEERS):
        later = e > here[0]
        weights[e] = jnp.where(later, w, 0.0)
        w = jnp.where(later, w * got[e, 0:1, :], w)
    keep, _ = gains(span[...])
    carry = masked(carry_ref[...], here[0] * ROWS, begin)
    f = jnp.ones((CHUNKS, K), F32)
    for i in reversed(range(STEPS)):
        decay = column(carry, i) * keep
        to = pl.ds(i, CHUNKS, stride=STEPS)
        suffix[to, :] = f
        decays[to, :] = decay
        f = decay * f
    start = pl.multiple_of((core[0] * 4 + za[0] * 2) * STEPS, QUARTER)
    own_decay[...] = decays[pl.ds(start, QUARTER), :]


def sum_kernel(weights, late, own_decay, mine, other, out, p):
    p[...] = mine[...] + other[...]
    r = jnp.zeros((CHUNKS, K), F32)
    m = jnp.ones((CHUNKS, K), F32)
    for i in reversed(range(FINE)):
        decay = rows(own_decay, i, FINE)
        r = decay * (rows(p, i, FINE) + r)
        m = decay * m
    entries = [jnp.zeros((1, K), F32)]
    for j in reversed(range(CHUNKS)):
        entries.append(m[j : j + 1] * entries[-1] + r[j : j + 1])
    total = entries.pop()
    r = jnp.concatenate(entries[::-1], axis=0)
    for i in reversed(range(FINE)):
        adjoint = rows(p, i, FINE) + r
        out[pl.ds(i, CHUNKS, stride=FINE), :] = adjoint
        r = rows(own_decay, i, FINE) * adjoint
    late = late[...]
    entry = jnp.sum(weights[...] * (late[:, 0:1, :] + late[:, 1:2, :]), axis=0)
    out[QUARTER:PART, :] = jnp.concatenate(
        [total, entry, jnp.zeros((PART - QUARTER - 2, K), F32)], axis=0
    )


def finish_kernel(za, span, d, chunk, suffix, mine, other, out):
    _, gain = gains(span[...])
    tail = (mine[0, QUARTER:PART, :] + mine[1, QUARTER:PART, :]) + (
        other[0, QUARTER:PART, :] + other[1, QUARTER:PART, :]
    )
    entry = tail[1:2]
    for quarter in reversed(range(4)):
        own = za[0] == quarter % 2

        def part(at):
            return jnp.where(own, mine[quarter // 2, at, :], other[quarter // 2, at, :])

        for j in (1, 0):
            at = pl.ds((quarter * 2 + j) * STEPS, STEPS)
            entering = entry if j else chunk[0, quarter * 2 + 1 : quarter * 2 + 2, :] * entry
            adjoint = part(pl.ds(j * STEPS, STEPS)) + suffix[at, :] * entering
            out[at, :] = gain * adjoint + d[at, :].astype(F32)
        entry = chunk[0, quarter * 2 : quarter * 2 + 1, :] * entering + part(pl.ds(QUARTER, 8))[0:1]


def local(x, d, coupling, assay, shift, span, carry, begin):
    here = lax.axis_index(BINS)[None]
    za, core = lax.axis_index("za")[None], lax.axis_index("core")[None]
    span = span.reshape(1, K)
    carry = carry.reshape(CHUNKS, STEPS)
    wide, quarter = ((ROWS, K), F32), ((QUARTER, K), F32)
    packed = ((3 * K, 2 * TRACKS), BF16)
    pad = VMEM((CHUNKS * PAD, K), F32)
    chunk, sent, shard = call(
        ends_kernel,
        [SMEM] + [HBM] * 7,
        [((3, CHUNKS, K), F32), ((PEERS, 3, K), F32), ((SHARD, K), F32)],
        [
            SMEM((3,), jnp.int32),
            VMEM((1, K), F32),
            VMEM((CHUNKS, STEPS), F32),
            VMEM((TRACKS // K, K), jnp.int32),
            VMEM((TRACKS, K), BF16),
            VMEM((ROWS, K), BF16),
            VMEM((ROWS, K), BF16),
            VMEM((SHARD, K), F32),
            pad,
            pad,
            pltpu.SemaphoreType.DMA((8,)),
        ],
        vmem=60,
        spaces=[VMEM, VMEM, HBM],
    )(here, begin, span, carry, assay.reshape(TRACKS // K, K), coupling, x, d)
    got = lax.all_to_all(sent, BINS, 0, 0, tiled=True)

    swap = [(0, 1), (1, 0)]
    mine = lax.all_gather(shard, "core")
    other = lax.ppermute(mine, "za", swap)
    latent, moved, product, shift_t, both = call(
        prepare_kernel,
        [SMEM] * 4 + [VMEM] * 7,
        [quarter, quarter, quarter, ((QUARTER, K), BF16), packed],
        [VMEM(*quarter), VMEM(*quarter)],
    )(here, za, core, begin, span, carry, x, d, chunk, shift, mine)

    pulled, sent = call(
        tracks_kernel,
        [SMEM] + [VMEM] * 7,
        [quarter, ((2 * PEERS, 1, K), F32)],
        [VMEM(*packed)],
    )(here, got, latent, moved, product, shift_t, both, other)
    late = lax.all_to_all(sent, BINS + ("zb",), 0, 0, tiled=True)
    received = lax.ppermute(pulled, "zb", swap)
    weights, suffix, own_decay = call(
        later_kernel,
        [SMEM] * 4 + [VMEM] * 3,
        [((PEERS, 1, K), F32), wide, quarter],
        [VMEM(*wide)],
    )(here, za, core, begin, span, carry, got)
    (part,) = call(sum_kernel, [VMEM] * 5, [((PART, K), F32)], [VMEM(*quarter)])(
        weights, late.reshape(PEERS, 2, K), own_decay, pulled, received
    )
    other = lax.ppermute(part, "za", swap)
    mine = lax.all_gather(part, "core")
    other = lax.all_gather(other, "core")
    (out,) = call(finish_kernel, [SMEM] + [VMEM] * 6, [wide])(
        za, span, d, chunk, suffix, mine, other
    )
    return out


def solution(mesh):
    fine = Mesh(mesh.devices.reshape(8, 2, 4, 2, 2, 2), ("y", "zh", "x", "zb", "za", "core"))
    in_specs = (
        P(BINS, None),
        P(BINS, None),
        P(VIEW, None),
        P(VIEW),
        P(None, BINS),
        P(),
        P(BINS),
        P(),
    )
    return jax.shard_map(
        local, mesh=fine, in_specs=in_specs, out_specs=P(BINS, None), check_vma=False
    )
```

```python
import jax
import jax.numpy as jnp
from jax import lax
from jax.experimental import pallas as pl
from jax.experimental.pallas import tpu as pltpu
from jax.sharding import Mesh, PartitionSpec as P

ROWS, QUARTER, K, CHUNKS, STEPS = 1024, 256, 128, 8, 128
PEERS, NVIEW, TRACKS = 64, 8, 640
SHARD = TRACKS + 8
FINE = 32
PAD = STEPS + 8
PART = QUARTER + 8
BINS, VIEW = "bins", ("zb", "za", "core")
FIRST = 38
ORDER = [(FIRST + i) % PEERS for i in range(PEERS)]
VMEM, SMEM, HBM = pltpu.VMEM, pltpu.SMEM, pltpu.HBM
F32, BF16 = jnp.float32, jnp.bfloat16


def spec(space):
    return pl.BlockSpec(memory_space=space)


def call(body, ins, outs, scratch=(), vmem=16, spaces=None):
    return pl.pallas_call(
        body,
        in_specs=[spec(s) for s in ins],
        out_specs=[spec(s) for s in spaces or [VMEM] * len(outs)],
        out_shape=[jax.ShapeDtypeStruct(shape, dtype) for shape, dtype in outs],
        scratch_shapes=list(scratch),
        compiler_params=pltpu.CompilerParams(vmem_limit_bytes=vmem * 1024 * 1024),
    )


def gains(span):
    forget = 1.0 / span
    return 1.0 - forget, jnp.sqrt(forget * (2.0 - forget))


def masked(carry, first, begin_ref):
    m = carry.shape[1]
    at = (
        first
        + lax.broadcasted_iota(jnp.int32, carry.shape, 0) * m
        + lax.broadcasted_iota(jnp.int32, carry.shape, 1)
    )
    begins = (at == begin_ref[0]) | (at == begin_ref[1]) | (at == begin_ref[2])
    return jnp.where(begins, 0.0, carry)


def column(carry, i):
    return jnp.broadcast_to(carry[:, i : i + 1], (CHUNKS, K))


def rows(ref, i, stride):
    return ref[pl.ds(i, CHUNKS, stride=stride), :]


def ends_kernel(
    here, begin_hbm, span_hbm, carry_hbm, assay_hbm, coupling_hbm, x_hbm, d_hbm,
    chunk, sent, shard_hbm,
    begin, span, carry_ref, assay, coupling, x, d, shard, xs, ds, sems,
):
    pairs = [
        (coupling_hbm, coupling),
        (assay_hbm, assay),
        (carry_hbm, carry_ref),
        (span_hbm, span),
        (begin_hbm, begin),
        (x_hbm, x),
        (d_hbm, d),
    ]
    copies = [pltpu.make_async_copy(a, b, sems.at[i]) for i, (a, b) in enumerate(pairs)]
    for copy in copies:
        copy.start()
    copies[0].wait()
    copies[1].wait()
    rest = jnp.zeros((SHARD - TRACKS - TRACKS // K, K), jnp.int32)
    shard[0:TRACKS, :] = coupling[...].astype(F32)
    shard[TRACKS:SHARD, :] = jnp.concatenate([assay[...], rest], axis=0).astype(F32)
    leave = pltpu.make_async_copy(shard, shard_hbm, sems.at[len(pairs)])
    leave.start()
    for copy in copies[2:]:
        copy.wait()
    keep, gain = gains(span[...])
    carry = masked(carry_ref[...], here[0] * ROWS, begin)
    for j in range(CHUNKS):
        at, to = pl.ds(j * STEPS, STEPS), pl.ds(j * PAD, STEPS)
        xs[to, :] = gain * x[at, :].astype(F32)
        ds[to, :] = gain * d[at, :].astype(F32)
    half = STEPS // 2
    ends = []
    for first in (0, half):
        z, v = rows(xs, first, PAD), rows(ds, first, PAD)
        m = column(carry, first) * keep
        for i in range(first + 1, first + half):
            decay = column(carry, i) * keep
            z = decay * z + rows(xs, i, PAD)
            v = decay * v + rows(ds, i, PAD)
            m = decay * m
        ends.append((m, z, v))
    (m0, z0, v0), (m1, z1, v1) = ends
    m, z, v = m0 * m1, m1 * z0 + z1, m1 * v0 + v1
    chunk[0] = m
    chunk[1] = z
    chunk[2] = v
    mt, zt, vt = m[0:1], z[0:1], v[0:1]
    for j in range(1, CHUNKS):
        mj = m[j : j + 1]
        mt, zt, vt = mj * mt, mj * zt + z[j : j + 1], mj * vt + v[j : j + 1]
    sent[...] = jnp.broadcast_to(jnp.concatenate([mt, zt, vt], axis=0)[None], sent.shape)
    leave.wait()


def prepare_kernel(
    here, za, core, begin, span, carry_ref, x, d, chunk, shift, mine,
    latent, moved, product, shift_t, both, xs, ds,
):
    at = core[0] * 4 + za[0] * 2
    start = pl.multiple_of(at * STEPS, QUARTER)
    keep, gain = gains(span[...])
    pair = masked(carry_ref[pl.ds(at, 2), :], here[0] * ROWS + start, begin)
    carry = jnp.concatenate(
        [pair[j : j + 1, i : i + FINE] for j in range(2) for i in range(0, STEPS, FINE)], axis=0
    )
    xs[...] = gain * x[pl.ds(start, QUARTER), :].astype(F32)
    ds[...] = gain * d[pl.ds(start, QUARTER), :].astype(F32)
    z, v = rows(xs, 0, FINE), rows(ds, 0, FINE)
    m = column(carry, 0) * keep
    for i in range(1, FINE):
        decay = column(carry, i) * keep
        z = decay * z + rows(xs, i, FINE)
        v = decay * v + rows(ds, i, FINE)
        m = decay * m
    q, ez, ev = jnp.ones((1, K), F32), jnp.zeros((1, K), F32), jnp.zeros((1, K), F32)
    for j in range(CHUNKS - 2):
        before = j < at
        mj, zj, vj = (chunk[i, j : j + 1, :] for i in range(3))
        q = jnp.where(before, mj * q, q)
        ez = jnp.where(before, mj * ez + zj, ez)
        ev = jnp.where(before, mj * ev + vj, ev)
    qs, zs, vs = [q], [ez], [ev]
    for j in range(CHUNKS - 1):
        mj = m[j : j + 1]
        qs.append(mj * qs[-1])
        zs.append(mj * zs[-1] + z[j : j + 1])
        vs.append(mj * vs[-1] + v[j : j + 1])
    q, z, v = (jnp.concatenate(a, axis=0) for a in (qs, zs, vs))
    for i in range(FINE):
        decay = column(carry, i) * keep
        q = decay * q
        z = decay * z + rows(xs, i, FINE)
        v = decay * v + rows(ds, i, FINE)
        to = pl.ds(i, CHUNKS, stride=FINE)
        product[to, :] = q
        latent[to, :] = z
        moved[to, :] = v
    s = shift[:, pl.ds(start, QUARTER)]
    hi = s.astype(BF16).astype(F32)
    mid = (s - hi).astype(BF16).astype(F32)
    low = s - hi - mid
    blank = jnp.zeros((K - 3 * NVIEW, QUARTER), F32)
    shift_t[...] = jnp.concatenate([hi, mid, low, blank], axis=0).T.astype(BF16)
    couple(mine, both)


def couple(shards, both):
    for side in range(2):
        ref = shards.at[side]
        at = pl.ds(side * TRACKS, TRACKS)
        w = ref[0:TRACKS, :]
        both[0:K, at] = w.T.astype(BF16)
        both[2 * K : 3 * K, at] = jnp.concatenate(
            [w[i : i + K] for i in range(0, TRACKS, K)], axis=1
        ).astype(BF16)
        assay = ref[TRACKS:SHARD, :]
        assay = jnp.concatenate([assay[i : i + 1] for i in range(TRACKS // K)], axis=1)
        view = lax.broadcasted_iota(jnp.int32, (NVIEW, TRACKS), 0).astype(F32)
        member = (assay == view).astype(F32)
        blank = jnp.zeros((K - 3 * NVIEW, TRACKS), F32)
        both[K : 2 * K, at] = jnp.concatenate([member] * 3 + [blank], axis=0).astype(BF16)


def tracks_kernel(
    here, got, latent_ref, moved_ref, product_ref, shift_t, mine, other,
    pulled, sent, theirs,
):
    couple(other, theirs)
    ez = jnp.zeros((1, K), F32)
    ev = jnp.zeros((1, K), F32)
    for e in range(PEERS - 1):
        at = (e - FIRST) % PEERS
        m, z, v = got[at, 0:1, :], got[at, 1:2, :], got[at, 2:3, :]
        earlier = e < here[0]
        ez = jnp.where(earlier, m * ez + z, ez)
        ev = jnp.where(earlier, m * ev + v, ev)
    product = product_ref[...]
    latent = (latent_ref[...] + product * ez).astype(BF16)
    latent = jnp.concatenate([latent, shift_t[...]], axis=1)
    moved = (moved_ref[...] + product * ev).astype(BF16)
    p = jnp.zeros((QUARTER, K), F32)
    for side in range(4):
        both, at = (mine, theirs)[side // 2], pl.ds(side % 2 * TRACKS, TRACKS)
        log_rate = jnp.dot(latent, both[0 : 2 * K, at], preferred_element_type=F32)
        along = jnp.dot(moved, both[0:K, at], preferred_element_type=F32)
        weighted = (jnp.exp(log_rate) * along).astype(BF16)
        blocks = both[2 * K : 3 * K, at]
        coupling = jnp.concatenate([blocks[:, i : i + K] for i in range(0, TRACKS, K)], axis=0)
        p = p + jnp.dot(weighted, coupling, preferred_element_type=F32)
    pulled[...] = p
    total = jnp.sum(product * p, axis=0, keepdims=True)
    sent[...] = jnp.broadcast_to(total[None], sent.shape)


def later_kernel(here, za, core, begin, span, carry_ref, got, weights, suffix, own_decay, decays):
    w = jnp.ones((1, K), F32)
    for e in range(PEERS):
        later = e > here[0]
        weights[e] = jnp.where(later, w, 0.0)
        w = jnp.where(later, w * got[(e - FIRST) % PEERS, 0:1, :], w)
    keep, _ = gains(span[...])
    carry = masked(carry_ref[...], here[0] * ROWS, begin)
    f = jnp.ones((CHUNKS, K), F32)
    for i in reversed(range(STEPS)):
        decay = column(carry, i) * keep
        to = pl.ds(i, CHUNKS, stride=STEPS)
        suffix[to, :] = f
        decays[to, :] = decay
        f = decay * f
    start = pl.multiple_of((core[0] * 4 + za[0] * 2) * STEPS, QUARTER)
    own_decay[...] = decays[pl.ds(start, QUARTER), :]


def sum_kernel(weights, late, own_decay, mine, other, out, p):
    p[...] = mine[...] + other[...]
    r = jnp.zeros((CHUNKS, K), F32)
    m = jnp.ones((CHUNKS, K), F32)
    for i in reversed(range(FINE)):
        decay = rows(own_decay, i, FINE)
        r = decay * (rows(p, i, FINE) + r)
        m = decay * m
    entries = [jnp.zeros((1, K), F32)]
    for j in reversed(range(CHUNKS)):
        entries.append(m[j : j + 1] * entries[-1] + r[j : j + 1])
    total = entries.pop()
    r = jnp.concatenate(entries[::-1], axis=0)
    for i in reversed(range(FINE)):
        adjoint = rows(p, i, FINE) + r
        out[pl.ds(i, CHUNKS, stride=FINE), :] = adjoint
        r = rows(own_decay, i, FINE) * adjoint
    late = late[...]
    entry = jnp.sum(weights[...] * (late[:, 0:1, :] + late[:, 1:2, :]), axis=0)
    out[QUARTER:PART, :] = jnp.concatenate(
        [total, entry, jnp.zeros((PART - QUARTER - 2, K), F32)], axis=0
    )


def finish_kernel(za, span, d, chunk, suffix, mine, other, out):
    _, gain = gains(span[...])
    tail = (mine[0, QUARTER:PART, :] + mine[1, QUARTER:PART, :]) + (
        other[0, QUARTER:PART, :] + other[1, QUARTER:PART, :]
    )
    entry = tail[1:2]
    for quarter in reversed(range(4)):
        own = za[0] == quarter % 2

        def part(at):
            return jnp.where(own, mine[quarter // 2, at, :], other[quarter // 2, at, :])

        for j in (1, 0):
            at = pl.ds((quarter * 2 + j) * STEPS, STEPS)
            entering = entry if j else chunk[0, quarter * 2 + 1 : quarter * 2 + 2, :] * entry
            adjoint = part(pl.ds(j * STEPS, STEPS)) + suffix[at, :] * entering
            out[at, :] = gain * adjoint + d[at, :].astype(F32)
        entry = chunk[0, quarter * 2 : quarter * 2 + 1, :] * entering + part(pl.ds(QUARTER, 8))[0:1]


def local(x, d, coupling, assay, shift, span, carry, begin):
    here = lax.axis_index(BINS)[None]
    za, core = lax.axis_index("za")[None], lax.axis_index("core")[None]
    span = span.reshape(1, K)
    carry = carry.reshape(CHUNKS, STEPS)
    wide, quarter = ((ROWS, K), F32), ((QUARTER, K), F32)
    packed = ((3 * K, 2 * TRACKS), BF16)
    pad = VMEM((CHUNKS * PAD, K), F32)
    chunk, sent, shard = call(
        ends_kernel,
        [SMEM] + [HBM] * 7,
        [((3, CHUNKS, K), F32), ((PEERS, 3, K), F32), ((SHARD, K), F32)],
        [
            SMEM((3,), jnp.int32),
            VMEM((1, K), F32),
            VMEM((CHUNKS, STEPS), F32),
            VMEM((TRACKS // K, K), jnp.int32),
            VMEM((TRACKS, K), BF16),
            VMEM((ROWS, K), BF16),
            VMEM((ROWS, K), BF16),
            VMEM((SHARD, K), F32),
            pad,
            pad,
            pltpu.SemaphoreType.DMA((8,)),
        ],
        vmem=60,
        spaces=[VMEM, VMEM, HBM],
    )(here, begin, span, carry, assay.reshape(TRACKS // K, K), coupling, x, d)
    got = lax.all_to_all(sent, BINS, 0, 0, axis_index_groups=[ORDER], tiled=True)

    swap = [(0, 1), (1, 0)]
    mine = lax.all_gather(shard, "core")
    other = lax.ppermute(mine, "za", swap)
    latent, moved, product, shift_t, both = call(
        prepare_kernel,
        [SMEM] * 4 + [VMEM] * 7,
        [quarter, quarter, quarter, ((QUARTER, K), BF16), packed],
        [VMEM(*quarter), VMEM(*quarter)],
    )(here, za, core, begin, span, carry, x, d, chunk, shift, mine)

    pulled, sent = call(
        tracks_kernel,
        [SMEM] + [VMEM] * 7,
        [quarter, ((2 * PEERS, 1, K), F32)],
        [VMEM(*packed)],
    )(here, got, latent, moved, product, shift_t, both, other)
    late = lax.all_to_all(sent, (BINS, "zb"), 0, 0, tiled=True)
    received = lax.ppermute(pulled, "zb", swap)
    weights, suffix, own_decay = call(
        later_kernel,
        [SMEM] * 4 + [VMEM] * 3,
        [((PEERS, 1, K), F32), wide, quarter],
        [VMEM(*wide)],
    )(here, za, core, begin, span, carry, got)
    (part,) = call(sum_kernel, [VMEM] * 5, [((PART, K), F32)], [VMEM(*quarter)])(
        weights, late.reshape(PEERS, 2, K), own_decay, pulled, received
    )
    other = lax.ppermute(part, "za", swap)
    mine = lax.all_gather(part, "core")
    other = lax.all_gather(other, "core")
    (out,) = call(finish_kernel, [SMEM] + [VMEM] * 6, [wide])(
        za, span, d, chunk, suffix, mine, other
    )
    return out


def solution(mesh):
    fine = Mesh(mesh.devices.reshape(PEERS, 2, 2, 2), (BINS, *VIEW))
    in_specs = (
        P(BINS, None),
        P(BINS, None),
        P(VIEW, None),
        P(VIEW),
        P(None, BINS),
        P(),
        P(BINS),
        P(),
    )
    return jax.shard_map(
        local, mesh=fine, in_specs=in_specs, out_specs=P(BINS, None), check_vma=False
    )
```

```python
import jax
import jax.numpy as jnp
from jax import lax
from jax.experimental import pallas as pl
from jax.experimental.pallas import tpu as pltpu
from jax.sharding import Mesh, PartitionSpec as P

ROWS, QUARTER, K, CHUNKS, STEPS = 1024, 256, 128, 8, 128
PEERS, NVIEW, TRACKS = 64, 8, 640
SHARD = TRACKS + 8
FINE = 32
PAD = STEPS + 8
PART = QUARTER + 8
BINS, VIEW = "bins", ("zb", "za", "core")
FIRST = 38
ORDER = [(FIRST + i) % PEERS for i in range(PEERS)]
VMEM, SMEM, HBM = pltpu.VMEM, pltpu.SMEM, pltpu.HBM
F32, BF16 = jnp.float32, jnp.bfloat16


def spec(space):
    return pl.BlockSpec(memory_space=space)


def call(body, ins, outs, scratch=(), vmem=16, spaces=None):
    return pl.pallas_call(
        body,
        in_specs=[spec(s) for s in ins],
        out_specs=[spec(s) for s in spaces or [VMEM] * len(outs)],
        out_shape=[jax.ShapeDtypeStruct(shape, dtype) for shape, dtype in outs],
        scratch_shapes=list(scratch),
        compiler_params=pltpu.CompilerParams(vmem_limit_bytes=vmem * 1024 * 1024),
    )


def gains(span):
    forget = 1.0 / span
    return 1.0 - forget, jnp.sqrt(forget * (2.0 - forget))


def masked(carry, first, begin_ref):
    m = carry.shape[1]
    at = (
        first
        + lax.broadcasted_iota(jnp.int32, carry.shape, 0) * m
        + lax.broadcasted_iota(jnp.int32, carry.shape, 1)
    )
    begins = (at == begin_ref[0]) | (at == begin_ref[1]) | (at == begin_ref[2])
    return jnp.where(begins, 0.0, carry)


def column(carry, i):
    return jnp.broadcast_to(carry[:, i : i + 1], (CHUNKS, K))


def rows(ref, i, stride):
    return ref[pl.ds(i, CHUNKS, stride=stride), :]


def ends_kernel(
    here, za, core, begin_hbm, span_hbm, carry_hbm, assay_hbm, coupling_hbm, x_hbm, d_hbm,
    chunk, sent, shard_hbm, scaled_hbm,
    begin, span, carry_ref, assay, coupling, x, d, shard, xs, ds, sems,
):
    pairs = [
        (coupling_hbm, coupling),
        (assay_hbm, assay),
        (carry_hbm, carry_ref),
        (span_hbm, span),
        (begin_hbm, begin),
        (x_hbm, x),
        (d_hbm, d),
    ]
    copies = [pltpu.make_async_copy(a, b, sems.at[i]) for i, (a, b) in enumerate(pairs)]
    for copy in copies:
        copy.start()
    copies[0].wait()
    copies[1].wait()
    rest = jnp.zeros((SHARD - TRACKS - TRACKS // K, K), jnp.int32)
    shard[0:TRACKS, :] = coupling[...].astype(F32)
    shard[TRACKS:SHARD, :] = jnp.concatenate([assay[...], rest], axis=0).astype(F32)
    leaves = [pltpu.make_async_copy(shard, shard_hbm, sems.at[len(pairs)])]
    leaves[0].start()
    for copy in copies[2:]:
        copy.wait()
    keep, gain = gains(span[...])
    carry = masked(carry_ref[...], here[0] * ROWS, begin)
    for j in range(CHUNKS):
        at, to = pl.ds(j * STEPS, STEPS), pl.ds(j * PAD, STEPS)
        xs[to, :] = gain * x[at, :].astype(F32)
        ds[to, :] = gain * d[at, :].astype(F32)
    for j in range(2):
        at = pl.multiple_of((core[0] * 4 + za[0] * 2 + j) * PAD, 8)
        for k, ref in enumerate((xs, ds)):
            to = scaled_hbm.at[k, pl.ds(j * STEPS, STEPS), :]
            sem = sems.at[len(pairs) + len(leaves)]
            leaves.append(pltpu.make_async_copy(ref.at[pl.ds(at, STEPS), :], to, sem))
            leaves[-1].start()
    chunk[3] = carry
    chunk[4] = jnp.broadcast_to(keep, (CHUNKS, K))
    chunk[5] = jnp.broadcast_to(gain, (CHUNKS, K))
    half = STEPS // 2
    ends = []
    for first in (0, half):
        z, v = rows(xs, first, PAD), rows(ds, first, PAD)
        m = column(carry, first) * keep
        for i in range(first + 1, first + half):
            decay = column(carry, i) * keep
            z = decay * z + rows(xs, i, PAD)
            v = decay * v + rows(ds, i, PAD)
            m = decay * m
        ends.append((m, z, v))
    (m0, z0, v0), (m1, z1, v1) = ends
    m, z, v = m0 * m1, m1 * z0 + z1, m1 * v0 + v1
    chunk[0] = m
    chunk[1] = z
    chunk[2] = v
    mt, zt, vt = m[0:1], z[0:1], v[0:1]
    for j in range(1, CHUNKS):
        mj = m[j : j + 1]
        mt, zt, vt = mj * mt, mj * zt + z[j : j + 1], mj * vt + v[j : j + 1]
    sent[...] = jnp.broadcast_to(jnp.concatenate([mt, zt, vt], axis=0)[None], sent.shape)
    for copy in leaves:
        copy.wait()


def prepare_kernel(
    za, core, chunk, scaled, shift, shard, latent, moved, product, shift_t, mine
):
    mine[...] = shard[...]
    at = core[0] * 4 + za[0] * 2
    start = pl.multiple_of(at * STEPS, QUARTER)
    pair, keep = chunk[3, pl.ds(at, 2), :], chunk[4, 0:1, :]
    carry = jnp.concatenate(
        [pair[j : j + 1, i : i + FINE] for j in range(2) for i in range(0, STEPS, FINE)], axis=0
    )
    xs, ds = scaled.at[0], scaled.at[1]
    z, v = rows(xs, 0, FINE), rows(ds, 0, FINE)
    m = column(carry, 0) * keep
    for i in range(1, FINE):
        decay = column(carry, i) * keep
        z = decay * z + rows(xs, i, FINE)
        v = decay * v + rows(ds, i, FINE)
        m = decay * m
    q, ez, ev = jnp.ones((1, K), F32), jnp.zeros((1, K), F32), jnp.zeros((1, K), F32)
    for j in range(CHUNKS - 2):
        before = j < at
        mj, zj, vj = (chunk[i, j : j + 1, :] for i in range(3))
        q = jnp.where(before, mj * q, q)
        ez = jnp.where(before, mj * ez + zj, ez)
        ev = jnp.where(before, mj * ev + vj, ev)
    qs, zs, vs = [q], [ez], [ev]
    for j in range(CHUNKS - 1):
        mj = m[j : j + 1]
        qs.append(mj * qs[-1])
        zs.append(mj * zs[-1] + z[j : j + 1])
        vs.append(mj * vs[-1] + v[j : j + 1])
    q, z, v = (jnp.concatenate(a, axis=0) for a in (qs, zs, vs))
    for i in range(FINE):
        decay = column(carry, i) * keep
        q = decay * q
        z = decay * z + rows(xs, i, FINE)
        v = decay * v + rows(ds, i, FINE)
        to = pl.ds(i, CHUNKS, stride=FINE)
        product[to, :] = q
        latent[to, :] = z
        moved[to, :] = v
    s = shift[:, pl.ds(start, QUARTER)]
    hi = s.astype(BF16).astype(F32)
    mid = (s - hi).astype(BF16).astype(F32)
    low = s - hi - mid
    blank = jnp.zeros((K - 3 * NVIEW, QUARTER), F32)
    shift_t[...] = jnp.concatenate([hi, mid, low, blank], axis=0).T.astype(BF16)


def couple_kernel(mine, other, both):
    for side in range(4):
        ref = (mine, other)[side // 2].at[side % 2]
        at = pl.ds(side * TRACKS, TRACKS)
        w = ref[0:TRACKS, :]
        both[0:K, at] = w.T.astype(BF16)
        both[2 * K : 3 * K, at] = jnp.concatenate(
            [w[i : i + K] for i in range(0, TRACKS, K)], axis=1
        ).astype(BF16)
        assay = ref[TRACKS:SHARD, :]
        assay = jnp.concatenate([assay[i : i + 1] for i in range(TRACKS // K)], axis=1)
        view = lax.broadcasted_iota(jnp.int32, (NVIEW, TRACKS), 0).astype(F32)
        member = (assay == view).astype(F32)
        blank = jnp.zeros((K - 3 * NVIEW, TRACKS), F32)
        both[K : 2 * K, at] = jnp.concatenate([member] * 3 + [blank], axis=0).astype(BF16)


def tracks_kernel(
    here, got, latent_ref, moved_ref, product_ref, shift_t, both,
    pulled, sent,
):
    ez = jnp.zeros((1, K), F32)
    ev = jnp.zeros((1, K), F32)
    for e in range(PEERS - 1):
        at = (e - FIRST) % PEERS
        m, z, v = got[at, 0:1, :], got[at, 1:2, :], got[at, 2:3, :]
        earlier = e < here[0]
        ez = jnp.where(earlier, m * ez + z, ez)
        ev = jnp.where(earlier, m * ev + v, ev)
    product = product_ref[...]
    latent = (latent_ref[...] + product * ez).astype(BF16)
    latent = jnp.concatenate([latent, shift_t[...]], axis=1)
    moved = (moved_ref[...] + product * ev).astype(BF16)
    p = jnp.zeros((QUARTER, K), F32)
    for side in range(4):
        at = pl.ds(side * TRACKS, TRACKS)
        log_rate = jnp.dot(latent, both[0 : 2 * K, at], preferred_element_type=F32)
        along = jnp.dot(moved, both[0:K, at], preferred_element_type=F32)
        weighted = (jnp.exp(log_rate) * along).astype(BF16)
        blocks = both[2 * K : 3 * K, at]
        coupling = jnp.concatenate([blocks[:, i : i + K] for i in range(0, TRACKS, K)], axis=0)
        p = p + jnp.dot(weighted, coupling, preferred_element_type=F32)
    pulled[...] = p
    total = jnp.sum(product * p, axis=0, keepdims=True)
    sent[...] = jnp.broadcast_to(total[None], sent.shape)


def later_kernel(here, za, core, chunk, got, weights, suffix, own_decay, decays):
    w = jnp.ones((1, K), F32)
    for e in range(PEERS):
        later = e > here[0]
        weights[e] = jnp.where(later, w, 0.0)
        w = jnp.where(later, w * got[(e - FIRST) % PEERS, 0:1, :], w)
    carry, keep = chunk[3], chunk[4, 0:1, :]
    f = jnp.ones((CHUNKS, K), F32)
    for i in reversed(range(STEPS)):
        decay = column(carry, i) * keep
        to = pl.ds(i, CHUNKS, stride=STEPS)
        suffix[to, :] = f
        decays[to, :] = decay
        f = decay * f
    start = pl.multiple_of((core[0] * 4 + za[0] * 2) * STEPS, QUARTER)
    own_decay[...] = decays[pl.ds(start, QUARTER), :]


def sum_kernel(weights, late, own_decay, mine, other, out, p):
    p[...] = mine[...] + other[...]
    r = jnp.zeros((CHUNKS, K), F32)
    m = jnp.ones((CHUNKS, K), F32)
    for i in reversed(range(FINE)):
        decay = rows(own_decay, i, FINE)
        r = decay * (rows(p, i, FINE) + r)
        m = decay * m
    entries = [jnp.zeros((1, K), F32)]
    for j in reversed(range(CHUNKS)):
        entries.append(m[j : j + 1] * entries[-1] + r[j : j + 1])
    total = entries.pop()
    r = jnp.concatenate(entries[::-1], axis=0)
    for i in reversed(range(FINE)):
        adjoint = rows(p, i, FINE) + r
        out[pl.ds(i, CHUNKS, stride=FINE), :] = adjoint
        r = rows(own_decay, i, FINE) * adjoint
    late = late[...]
    entry = jnp.sum(weights[...] * (late[:, 0:1, :] + late[:, 1:2, :]), axis=0)
    out[QUARTER:PART, :] = jnp.concatenate(
        [total, entry, jnp.zeros((PART - QUARTER - 2, K), F32)], axis=0
    )


def finish_kernel(za, d, chunk, suffix, mine, other, out):
    gain = chunk[5, 0:1, :]
    tail = (mine[0, QUARTER:PART, :] + mine[1, QUARTER:PART, :]) + (
        other[0, QUARTER:PART, :] + other[1, QUARTER:PART, :]
    )
    entry = tail[1:2]
    for quarter in reversed(range(4)):
        own = za[0] == quarter % 2

        def part(at):
            return jnp.where(own, mine[quarter // 2, at, :], other[quarter // 2, at, :])

        for j in (1, 0):
            at = pl.ds((quarter * 2 + j) * STEPS, STEPS)
            entering = entry if j else chunk[0, quarter * 2 + 1 : quarter * 2 + 2, :] * entry
            adjoint = part(pl.ds(j * STEPS, STEPS)) + suffix[at, :] * entering
            out[at, :] = gain * adjoint + d[at, :].astype(F32)
        entry = chunk[0, quarter * 2 : quarter * 2 + 1, :] * entering + part(pl.ds(QUARTER, 8))[0:1]


def local(x, d, coupling, assay, shift, span, carry, begin):
    here = lax.axis_index(BINS)[None]
    za, core = lax.axis_index("za")[None], lax.axis_index("core")[None]
    span = span.reshape(1, K)
    carry = carry.reshape(CHUNKS, STEPS)
    wide, quarter = ((ROWS, K), F32), ((QUARTER, K), F32)
    pad = VMEM((CHUNKS * PAD, K), F32)
    chunk, sent, shard, scaled = call(
        ends_kernel,
        [SMEM] * 3 + [HBM] * 7,
        [((6, CHUNKS, K), F32), ((PEERS, 3, K), F32), ((SHARD, K), F32), ((2, QUARTER, K), F32)],
        [
            SMEM((3,), jnp.int32),
            VMEM((1, K), F32),
            VMEM((CHUNKS, STEPS), F32),
            VMEM((TRACKS // K, K), jnp.int32),
            VMEM((TRACKS, K), BF16),
            VMEM((ROWS, K), BF16),
            VMEM((ROWS, K), BF16),
            VMEM((SHARD, K), F32),
            pad,
            pad,
            pltpu.SemaphoreType.DMA((12,)),
        ],
        vmem=60,
        spaces=[VMEM, VMEM, HBM, HBM],
    )(here, za, core, begin, span, carry, assay.reshape(TRACKS // K, K), coupling, x, d)
    got = lax.all_to_all(sent, BINS, 0, 0, axis_index_groups=[ORDER], tiled=True)

    swap = [(0, 1), (1, 0)]
    other = lax.ppermute(shard, "za", swap)
    latent, moved, product, shift_t, mine = call(
        prepare_kernel,
        [SMEM] * 2 + [VMEM] * 4,
        [quarter, quarter, quarter, ((QUARTER, K), BF16), ((SHARD, K), F32)],
    )(za, core, chunk, scaled, shift, shard)
    (both,) = call(couple_kernel, [VMEM] * 2, [((3 * K, 4 * TRACKS), BF16)])(
        *(lax.all_gather(s, "core") for s in (mine, other))
    )

    pulled, sent = call(
        tracks_kernel,
        [SMEM] + [VMEM] * 6,
        [quarter, ((2 * PEERS, 1, K), F32)],
    )(here, got, latent, moved, product, shift_t, both)
    late = lax.all_to_all(sent, (BINS, "zb"), 0, 0, tiled=True)
    received = lax.ppermute(pulled, "zb", swap)
    weights, suffix, own_decay = call(
        later_kernel,
        [SMEM] * 3 + [VMEM] * 2,
        [((PEERS, 1, K), F32), wide, quarter],
        [VMEM(*wide)],
    )(here, za, core, chunk, got)
    (part,) = call(sum_kernel, [VMEM] * 5, [((PART, K), F32)], [VMEM(*quarter)])(
        weights, late.reshape(PEERS, 2, K), own_decay, pulled, received
    )
    other = lax.ppermute(part, "za", swap)
    mine = lax.all_gather(part, "core")
    other = lax.all_gather(other, "core")
    (out,) = call(finish_kernel, [SMEM] + [VMEM] * 5, [wide])(
        za, d, chunk, suffix, mine, other
    )
    return out


def solution(mesh):
    fine = Mesh(mesh.devices.reshape(PEERS, 2, 2, 2), (BINS, *VIEW))
    in_specs = (
        P(BINS, None),
        P(BINS, None),
        P(VIEW, None),
        P(VIEW),
        P(None, BINS),
        P(),
        P(BINS),
        P(),
    )
    return jax.shard_map(
        local, mesh=fine, in_specs=in_specs, out_specs=P(BINS, None), check_vma=False
    )
```

```python
import jax
import jax.numpy as jnp
from jax import lax
from jax.experimental import pallas as pl
from jax.experimental.pallas import tpu as pltpu
from jax.sharding import Mesh, PartitionSpec as P

ROWS, QUARTER, K, CHUNKS, STEPS = 1024, 256, 128, 8, 128
PEERS, NVIEW, TRACKS = 64, 8, 640
SHARD = TRACKS + 8
FINE = 32
WIDE = FINE + 8
PAD = STEPS + 8
PART = QUARTER + 8
BINS, VIEW = "bins", ("zb", "za", "core")
FIRST = 38
ORDER = [(FIRST + i) % PEERS for i in range(PEERS)]
VMEM, SMEM, HBM = pltpu.VMEM, pltpu.SMEM, pltpu.HBM
F32, BF16 = jnp.float32, jnp.bfloat16


def spec(space):
    return pl.BlockSpec(memory_space=space)


def call(body, ins, outs, scratch=(), vmem=16, spaces=None):
    return pl.pallas_call(
        body,
        in_specs=[spec(s) for s in ins],
        out_specs=[spec(s) for s in spaces or [VMEM] * len(outs)],
        out_shape=[jax.ShapeDtypeStruct(shape, dtype) for shape, dtype in outs],
        scratch_shapes=list(scratch),
        compiler_params=pltpu.CompilerParams(vmem_limit_bytes=vmem * 1024 * 1024),
    )


def gains(span):
    forget = 1.0 / span
    return 1.0 - forget, jnp.sqrt(forget * (2.0 - forget))


def masked(carry, first, begin_ref):
    m = carry.shape[1]
    at = (
        first
        + lax.broadcasted_iota(jnp.int32, carry.shape, 0) * m
        + lax.broadcasted_iota(jnp.int32, carry.shape, 1)
    )
    begins = (at == begin_ref[0]) | (at == begin_ref[1]) | (at == begin_ref[2])
    return jnp.where(begins, 0.0, carry)


def column(carry, i):
    return jnp.broadcast_to(carry[:, i : i + 1], (CHUNKS, K))


def rows(ref, i, stride):
    return ref[pl.ds(i, CHUNKS, stride=stride), :]


def ends_kernel(
    here, begin_hbm, span_hbm, carry_hbm, assay_hbm, coupling_hbm, x_hbm, d_hbm,
    chunk, sent, shard_hbm,
    begin, span, carry_ref, assay, coupling, x, d, shard, xs, ds, sems,
):
    pairs = [
        (coupling_hbm, coupling),
        (assay_hbm, assay),
        (carry_hbm, carry_ref),
        (span_hbm, span),
        (begin_hbm, begin),
        (x_hbm, x),
        (d_hbm, d),
    ]
    copies = [pltpu.make_async_copy(a, b, sems.at[i]) for i, (a, b) in enumerate(pairs)]
    for copy in copies:
        copy.start()
    copies[0].wait()
    copies[1].wait()
    rest = jnp.zeros((SHARD - TRACKS - TRACKS // K, K), jnp.int32)
    shard[0:TRACKS, :] = coupling[...].astype(F32)
    shard[TRACKS:SHARD, :] = jnp.concatenate([assay[...], rest], axis=0).astype(F32)
    leave = pltpu.make_async_copy(shard, shard_hbm, sems.at[len(pairs)])
    leave.start()
    for copy in copies[2:]:
        copy.wait()
    keep, gain = gains(span[...])
    carry = masked(carry_ref[...], here[0] * ROWS, begin)
    for j in range(CHUNKS):
        at, to = pl.ds(j * STEPS, STEPS), pl.ds(j * PAD, STEPS)
        xs[to, :] = gain * x[at, :].astype(F32)
        ds[to, :] = gain * d[at, :].astype(F32)
    chunk[3] = carry
    chunk[4] = jnp.broadcast_to(keep, (CHUNKS, K))
    chunk[5] = jnp.broadcast_to(gain, (CHUNKS, K))
    half = STEPS // 2
    ends = []
    for first in (0, half):
        z, v = rows(xs, first, PAD), rows(ds, first, PAD)
        m = column(carry, first) * keep
        for i in range(first + 1, first + half):
            decay = column(carry, i) * keep
            z = decay * z + rows(xs, i, PAD)
            v = decay * v + rows(ds, i, PAD)
            m = decay * m
        ends.append((m, z, v))
    (m0, z0, v0), (m1, z1, v1) = ends
    m, z, v = m0 * m1, m1 * z0 + z1, m1 * v0 + v1
    chunk[0] = m
    chunk[1] = z
    chunk[2] = v
    mt, zt, vt = m[0:1], z[0:1], v[0:1]
    for j in range(1, CHUNKS):
        mj = m[j : j + 1]
        mt, zt, vt = mj * mt, mj * zt + z[j : j + 1], mj * vt + v[j : j + 1]
    sent[...] = jnp.broadcast_to(jnp.concatenate([mt, zt, vt], axis=0)[None], sent.shape)
    leave.wait()


def prepare_kernel(
    za, core, chunk, x, d, shift, shard, latent, moved, product, shift_t, mine, xs, ds
):
    mine[...] = shard[...]
    at = core[0] * 4 + za[0] * 2
    start = pl.multiple_of(at * STEPS, QUARTER)
    pair, keep, gain = chunk[3, pl.ds(at, 2), :], chunk[4, 0:1, :], chunk[5, 0:1, :]
    carry = jnp.concatenate(
        [pair[j : j + 1, i : i + FINE] for j in range(2) for i in range(0, STEPS, FINE)], axis=0
    )
    xs[...] = gain * x[pl.ds(start, QUARTER), :].astype(F32)
    ds[...] = gain * d[pl.ds(start, QUARTER), :].astype(F32)
    z, v = rows(xs, 0, FINE), rows(ds, 0, FINE)
    m = column(carry, 0) * keep
    for i in range(1, FINE):
        decay = column(carry, i) * keep
        z = decay * z + rows(xs, i, FINE)
        v = decay * v + rows(ds, i, FINE)
        m = decay * m
    q, ez, ev = jnp.ones((1, K), F32), jnp.zeros((1, K), F32), jnp.zeros((1, K), F32)
    for j in range(CHUNKS - 2):
        before = j < at
        mj, zj, vj = (chunk[i, j : j + 1, :] for i in range(3))
        q = jnp.where(before, mj * q, q)
        ez = jnp.where(before, mj * ez + zj, ez)
        ev = jnp.where(before, mj * ev + vj, ev)
    qs, zs, vs = [q], [ez], [ev]
    for j in range(CHUNKS - 1):
        mj = m[j : j + 1]
        qs.append(mj * qs[-1])
        zs.append(mj * zs[-1] + z[j : j + 1])
        vs.append(mj * vs[-1] + v[j : j + 1])
    q, z, v = (jnp.concatenate(a, axis=0) for a in (qs, zs, vs))
    for i in range(FINE):
        decay = column(carry, i) * keep
        q = decay * q
        z = decay * z + rows(xs, i, FINE)
        v = decay * v + rows(ds, i, FINE)
        to = pl.ds(i, CHUNKS, stride=FINE)
        product[to, :] = q
        latent[to, :] = z
        moved[to, :] = v
    s = shift[:, pl.ds(start, QUARTER)]
    hi = s.astype(BF16).astype(F32)
    mid = (s - hi).astype(BF16).astype(F32)
    low = s - hi - mid
    blank = jnp.zeros((K - 3 * NVIEW, QUARTER), F32)
    shift_t[...] = jnp.concatenate([hi, mid, low, blank], axis=0).T.astype(BF16)


def couple_kernel(mine, other, both):
    for side in range(4):
        ref = (mine, other)[side // 2].at[side % 2]
        at = pl.ds(side * TRACKS, TRACKS)
        w = ref[0:TRACKS, :]
        both[0:K, at] = w.T.astype(BF16)
        both[2 * K : 3 * K, at] = jnp.concatenate(
            [w[i : i + K] for i in range(0, TRACKS, K)], axis=1
        ).astype(BF16)
        assay = ref[TRACKS:SHARD, :]
        assay = jnp.concatenate([assay[i : i + 1] for i in range(TRACKS // K)], axis=1)
        view = lax.broadcasted_iota(jnp.int32, (NVIEW, TRACKS), 0).astype(F32)
        member = (assay == view).astype(F32)
        blank = jnp.zeros((K - 3 * NVIEW, TRACKS), F32)
        both[K : 2 * K, at] = jnp.concatenate([member] * 3 + [blank], axis=0).astype(BF16)


def tracks_kernel(
    here, got, latent_ref, moved_ref, product_ref, shift_t, both,
    pulled, sent,
):
    ez = jnp.zeros((1, K), F32)
    ev = jnp.zeros((1, K), F32)
    for e in range(PEERS - 1):
        at = (e - FIRST) % PEERS
        m, z, v = got[at, 0:1, :], got[at, 1:2, :], got[at, 2:3, :]
        earlier = e < here[0]
        ez = jnp.where(earlier, m * ez + z, ez)
        ev = jnp.where(earlier, m * ev + v, ev)
    product = product_ref[...]
    latent = (latent_ref[...] + product * ez).astype(BF16)
    latent = jnp.concatenate([latent, shift_t[...]], axis=1)
    moved = (moved_ref[...] + product * ev).astype(BF16)
    log_rate = jnp.dot(latent, both[0 : 2 * K, :], preferred_element_type=F32)
    along = jnp.dot(moved, both[0:K, :], preferred_element_type=F32)
    weighted = (jnp.exp(log_rate) * along).astype(BF16)
    blocks = both[2 * K : 3 * K, :]
    coupling = jnp.concatenate([blocks[:, i : i + K] for i in range(0, 4 * TRACKS, K)], axis=0)
    p = jnp.dot(weighted, coupling, preferred_element_type=F32)
    pulled[...] = p
    total = jnp.sum(product * p, axis=0, keepdims=True)
    sent[...] = jnp.broadcast_to(total[None], sent.shape)


def later_kernel(here, za, core, chunk, got, weights, suffix, own_decay, decays):
    w = jnp.ones((1, K), F32)
    for e in range(PEERS):
        later = e > here[0]
        weights[e] = jnp.where(later, w, 0.0)
        w = jnp.where(later, w * got[(e - FIRST) % PEERS, 0:1, :], w)
    carry, keep = chunk[3], chunk[4, 0:1, :]
    f = jnp.ones((CHUNKS, K), F32)
    for i in reversed(range(STEPS)):
        decay = column(carry, i) * keep
        to = pl.ds(i, CHUNKS, stride=STEPS)
        suffix[to, :] = f
        decays[to, :] = decay
        f = decay * f
    start = pl.multiple_of((core[0] * 4 + za[0] * 2) * STEPS, QUARTER)
    for j in range(CHUNKS):
        own_decay[pl.ds(j * WIDE, FINE), :] = decays[pl.ds(start + j * FINE, FINE), :]


def sum_kernel(weights, late, own_decay, mine, other, out, p):
    for j in range(CHUNKS):
        at = pl.ds(j * FINE, FINE)
        p[pl.ds(j * WIDE, FINE), :] = mine[at, :] + other[at, :]
    r = jnp.zeros((CHUNKS, K), F32)
    m = jnp.ones((CHUNKS, K), F32)
    for i in reversed(range(FINE)):
        decay = rows(own_decay, i, WIDE)
        r = decay * (rows(p, i, WIDE) + r)
        m = decay * m
    entries = [jnp.zeros((1, K), F32)]
    for j in reversed(range(CHUNKS)):
        entries.append(m[j : j + 1] * entries[-1] + r[j : j + 1])
    total = entries.pop()
    r = jnp.concatenate(entries[::-1], axis=0)
    for i in reversed(range(FINE)):
        adjoint = rows(p, i, WIDE) + r
        out[pl.ds(i, CHUNKS, stride=FINE), :] = adjoint
        r = rows(own_decay, i, WIDE) * adjoint
    late = late[...]
    entry = jnp.sum(weights[...] * (late[:, 0:1, :] + late[:, 1:2, :]), axis=0)
    out[QUARTER:PART, :] = jnp.concatenate(
        [total, entry, jnp.zeros((PART - QUARTER - 2, K), F32)], axis=0
    )


def finish_kernel(za, d, chunk, suffix, mine, other, out):
    gain = chunk[5, 0:1, :]
    tail = (mine[0, QUARTER:PART, :] + mine[1, QUARTER:PART, :]) + (
        other[0, QUARTER:PART, :] + other[1, QUARTER:PART, :]
    )
    entry = tail[1:2]
    for quarter in reversed(range(4)):
        own = za[0] == quarter % 2

        def part(at):
            return jnp.where(own, mine[quarter // 2, at, :], other[quarter // 2, at, :])

        for j in (1, 0):
            at = pl.ds((quarter * 2 + j) * STEPS, STEPS)
            entering = entry if j else chunk[0, quarter * 2 + 1 : quarter * 2 + 2, :] * entry
            adjoint = part(pl.ds(j * STEPS, STEPS)) + suffix[at, :] * entering
            out[at, :] = gain * adjoint + d[at, :].astype(F32)
        entry = chunk[0, quarter * 2 : quarter * 2 + 1, :] * entering + part(pl.ds(QUARTER, 8))[0:1]


def local(x, d, coupling, assay, shift, span, carry, begin):
    here = lax.axis_index(BINS)[None]
    za, core = lax.axis_index("za")[None], lax.axis_index("core")[None]
    span = span.reshape(1, K)
    carry = carry.reshape(CHUNKS, STEPS)
    wide, quarter = ((ROWS, K), F32), ((QUARTER, K), F32)
    pad = VMEM((CHUNKS * PAD, K), F32)
    chunk, sent, shard = call(
        ends_kernel,
        [SMEM] + [HBM] * 7,
        [((6, CHUNKS, K), F32), ((PEERS, 3, K), F32), ((SHARD, K), F32)],
        [
            SMEM((3,), jnp.int32),
            VMEM((1, K), F32),
            VMEM((CHUNKS, STEPS), F32),
            VMEM((TRACKS // K, K), jnp.int32),
            VMEM((TRACKS, K), BF16),
            VMEM((ROWS, K), BF16),
            VMEM((ROWS, K), BF16),
            VMEM((SHARD, K), F32),
            pad,
            pad,
            pltpu.SemaphoreType.DMA((8,)),
        ],
        vmem=60,
        spaces=[VMEM, VMEM, HBM],
    )(here, begin, span, carry, assay.reshape(TRACKS // K, K), coupling, x, d)
    got = lax.all_to_all(sent, BINS, 0, 0, axis_index_groups=[ORDER], tiled=True)

    swap = [(0, 1), (1, 0)]
    other = lax.ppermute(shard, "za", swap)
    latent, moved, product, shift_t, mine = call(
        prepare_kernel,
        [SMEM] * 2 + [VMEM] * 5,
        [quarter, quarter, quarter, ((QUARTER, K), BF16), ((SHARD, K), F32)],
        [VMEM(*quarter)] * 2,
    )(za, core, chunk, x, d, shift, shard)
    (both,) = call(couple_kernel, [VMEM] * 2, [((3 * K, 4 * TRACKS), BF16)])(
        *(lax.all_gather(s, "core") for s in (mine, other))
    )

    pulled, sent = call(
        tracks_kernel,
        [SMEM] + [VMEM] * 6,
        [quarter, ((2 * PEERS, 1, K), F32)],
        vmem=32,
    )(here, got, latent, moved, product, shift_t, both)
    late = lax.all_to_all(sent, (BINS, "zb"), 0, 0, tiled=True)
    received = lax.ppermute(pulled, "zb", swap)
    weights, suffix, own_decay = call(
        later_kernel,
        [SMEM] * 3 + [VMEM] * 2,
        [((PEERS, 1, K), F32), wide, ((CHUNKS * WIDE, K), F32)],
        [VMEM(*wide)],
    )(here, za, core, chunk, got)
    (part,) = call(sum_kernel, [VMEM] * 5, [((PART, K), F32)], [VMEM((CHUNKS * WIDE, K), F32)])(
        weights, late.reshape(PEERS, 2, K), own_decay, pulled, received
    )
    other = lax.ppermute(part, "za", swap)
    mine = lax.all_gather(part, "core")
    other = lax.all_gather(other, "core")
    (out,) = call(finish_kernel, [SMEM] + [VMEM] * 5, [wide])(
        za, d, chunk, suffix, mine, other
    )
    return out


def solution(mesh):
    fine = Mesh(mesh.devices.reshape(PEERS, 2, 2, 2), (BINS, *VIEW))
    in_specs = (
        P(BINS, None),
        P(BINS, None),
        P(VIEW, None),
        P(VIEW),
        P(None, BINS),
        P(),
        P(BINS),
        P(),
    )
    return jax.shard_map(
        local, mesh=fine, in_specs=in_specs, out_specs=P(BINS, None), check_vma=False
    )
```

```python
import jax
import jax.numpy as jnp
from jax import lax
from jax.experimental import pallas as pl
from jax.experimental.pallas import tpu as pltpu
from jax.sharding import Mesh, PartitionSpec as P

ROWS, QUARTER, K, CHUNKS, STEPS = 1024, 256, 128, 8, 128
PEERS, NVIEW, TRACKS = 64, 8, 640
SHARD = TRACKS + 8
FINE = 32
WIDE = FINE + 8
PAD = STEPS + 8
PART = QUARTER + 8
BINS, VIEW = "bins", ("zb", "za", "core")
FIRST = 38
ORDER = [(FIRST + i) % PEERS for i in range(PEERS)]
VMEM, SMEM, HBM = pltpu.VMEM, pltpu.SMEM, pltpu.HBM
F32, BF16 = jnp.float32, jnp.bfloat16


def spec(space):
    return pl.BlockSpec(memory_space=space)


def call(body, ins, outs, scratch=(), vmem=16, spaces=None):
    return pl.pallas_call(
        body,
        in_specs=[spec(s) for s in ins],
        out_specs=[spec(s) for s in spaces or [VMEM] * len(outs)],
        out_shape=[jax.ShapeDtypeStruct(shape, dtype) for shape, dtype in outs],
        scratch_shapes=list(scratch),
        compiler_params=pltpu.CompilerParams(vmem_limit_bytes=vmem * 1024 * 1024),
    )


def gains(span):
    forget = 1.0 / span
    return 1.0 - forget, jnp.sqrt(forget * (2.0 - forget))


def masked(carry, first, begin_ref):
    m = carry.shape[1]
    at = (
        first
        + lax.broadcasted_iota(jnp.int32, carry.shape, 0) * m
        + lax.broadcasted_iota(jnp.int32, carry.shape, 1)
    )
    begins = (at == begin_ref[0]) | (at == begin_ref[1]) | (at == begin_ref[2])
    return jnp.where(begins, 0.0, carry)


def column(carry, i):
    return jnp.broadcast_to(carry[:, i : i + 1], (CHUNKS, K))


def rows(ref, i, stride):
    return ref[pl.ds(i, CHUNKS, stride=stride), :]


def ends_kernel(
    here, begin_hbm, span_hbm, carry_hbm, assay_hbm, coupling_hbm, x_hbm, d_hbm,
    chunk, sent, shard_hbm,
    begin, span, carry_ref, assay, coupling, x, d, shard, xs, ds, sems,
):
    pairs = [
        (coupling_hbm, coupling),
        (assay_hbm, assay),
        (carry_hbm, carry_ref),
        (span_hbm, span),
        (begin_hbm, begin),
        (x_hbm, x),
        (d_hbm, d),
    ]
    copies = [pltpu.make_async_copy(a, b, sems.at[i]) for i, (a, b) in enumerate(pairs)]
    for copy in copies[5:] + copies[:5]:
        copy.start()
    copies[0].wait()
    copies[1].wait()
    rest = jnp.zeros((SHARD - TRACKS - TRACKS // K, K), jnp.int32)
    shard[0:TRACKS, :] = coupling[...].astype(F32)
    shard[TRACKS:SHARD, :] = jnp.concatenate([assay[...], rest], axis=0).astype(F32)
    leave = pltpu.make_async_copy(shard, shard_hbm, sems.at[len(pairs)])
    leave.start()
    for copy in copies[2:]:
        copy.wait()
    keep, gain = gains(span[...])
    carry = masked(carry_ref[...], here[0] * ROWS, begin)
    for j in range(CHUNKS):
        at, to = pl.ds(j * STEPS, STEPS), pl.ds(j * PAD, STEPS)
        xs[to, :] = gain * x[at, :].astype(F32)
        ds[to, :] = gain * d[at, :].astype(F32)
    chunk[3] = carry
    chunk[4] = jnp.broadcast_to(keep, (CHUNKS, K))
    chunk[5] = jnp.broadcast_to(gain, (CHUNKS, K))
    half = STEPS // 2
    ends = []
    for first in (0, half):
        z, v = rows(xs, first, PAD), rows(ds, first, PAD)
        m = column(carry, first) * keep
        for i in range(first + 1, first + half):
            decay = column(carry, i) * keep
            z = decay * z + rows(xs, i, PAD)
            v = decay * v + rows(ds, i, PAD)
            m = decay * m
        ends.append((m, z, v))
    (m0, z0, v0), (m1, z1, v1) = ends
    m, z, v = m0 * m1, m1 * z0 + z1, m1 * v0 + v1
    chunk[0] = m
    chunk[1] = z
    chunk[2] = v
    mt, zt, vt = m[0:1], z[0:1], v[0:1]
    for j in range(1, CHUNKS):
        mj = m[j : j + 1]
        mt, zt, vt = mj * mt, mj * zt + z[j : j + 1], mj * vt + v[j : j + 1]
    sent[...] = jnp.broadcast_to(jnp.concatenate([mt, zt, vt], axis=0)[None], sent.shape)
    leave.wait()


def prepare_kernel(
    za, core, chunk, x, d, shift, shard, latent, moved, product, shift_t, mine, xs, ds
):
    mine[...] = shard[...]
    at = core[0] * 4 + za[0] * 2
    start = pl.multiple_of(at * STEPS, QUARTER)
    pair, keep, gain = chunk[3, pl.ds(at, 2), :], chunk[4, 0:1, :], chunk[5, 0:1, :]
    carry = jnp.concatenate(
        [pair[j : j + 1, i : i + FINE] for j in range(2) for i in range(0, STEPS, FINE)], axis=0
    )
    xs[...] = gain * x[pl.ds(start, QUARTER), :].astype(F32)
    ds[...] = gain * d[pl.ds(start, QUARTER), :].astype(F32)
    z, v = rows(xs, 0, FINE), rows(ds, 0, FINE)
    m = column(carry, 0) * keep
    for i in range(1, FINE):
        decay = column(carry, i) * keep
        z = decay * z + rows(xs, i, FINE)
        v = decay * v + rows(ds, i, FINE)
        m = decay * m
    q, ez, ev = jnp.ones((1, K), F32), jnp.zeros((1, K), F32), jnp.zeros((1, K), F32)
    for j in range(CHUNKS - 2):
        before = j < at
        mj, zj, vj = (chunk[i, j : j + 1, :] for i in range(3))
        q = jnp.where(before, mj * q, q)
        ez = jnp.where(before, mj * ez + zj, ez)
        ev = jnp.where(before, mj * ev + vj, ev)
    qs, zs, vs = [q], [ez], [ev]
    for j in range(CHUNKS - 1):
        mj = m[j : j + 1]
        qs.append(mj * qs[-1])
        zs.append(mj * zs[-1] + z[j : j + 1])
        vs.append(mj * vs[-1] + v[j : j + 1])
    q, z, v = (jnp.concatenate(a, axis=0) for a in (qs, zs, vs))
    for i in range(FINE):
        decay = column(carry, i) * keep
        q = decay * q
        z = decay * z + rows(xs, i, FINE)
        v = decay * v + rows(ds, i, FINE)
        to = pl.ds(i, CHUNKS, stride=FINE)
        product[to, :] = q
        latent[to, :] = z
        moved[to, :] = v
    s = shift[:, pl.ds(start, QUARTER)]
    hi = s.astype(BF16).astype(F32)
    mid = (s - hi).astype(BF16).astype(F32)
    low = s - hi - mid
    blank = jnp.zeros((K - 3 * NVIEW, QUARTER), F32)
    shift_t[...] = jnp.concatenate([hi, mid, low, blank], axis=0).T.astype(BF16)


def couple_kernel(mine, other, both):
    for side in range(4):
        ref = (mine, other)[side // 2].at[side % 2]
        at = pl.ds(side * TRACKS, TRACKS)
        w = ref[0:TRACKS, :]
        both[0:K, at] = w.T.astype(BF16)
        both[2 * K : 3 * K, at] = jnp.concatenate(
            [w[i : i + K] for i in range(0, TRACKS, K)], axis=1
        ).astype(BF16)
        assay = ref[TRACKS:SHARD, :]
        assay = jnp.concatenate([assay[i : i + 1] for i in range(TRACKS // K)], axis=1)
        view = lax.broadcasted_iota(jnp.int32, (NVIEW, TRACKS), 0).astype(F32)
        member = (assay == view).astype(F32)
        blank = jnp.zeros((K - 3 * NVIEW, TRACKS), F32)
        both[K : 2 * K, at] = jnp.concatenate([member] * 3 + [blank], axis=0).astype(BF16)


def tracks_kernel(
    here, got, latent_ref, moved_ref, product_ref, shift_t, both,
    pulled, sent,
):
    ez = jnp.zeros((1, K), F32)
    ev = jnp.zeros((1, K), F32)
    for e in range(PEERS - 1):
        at = (e - FIRST) % PEERS
        m, z, v = got[at, 0:1, :], got[at, 1:2, :], got[at, 2:3, :]
        earlier = e < here[0]
        ez = jnp.where(earlier, m * ez + z, ez)
        ev = jnp.where(earlier, m * ev + v, ev)
    product = product_ref[...]
    latent = (latent_ref[...] + product * ez).astype(BF16)
    latent = jnp.concatenate([latent, shift_t[...]], axis=1)
    moved = (moved_ref[...] + product * ev).astype(BF16)
    log_rate = jnp.dot(latent, both[0 : 2 * K, :], preferred_element_type=F32)
    along = jnp.dot(moved, both[0:K, :], preferred_element_type=F32)
    weighted = (jnp.exp(log_rate) * along).astype(BF16)
    blocks = both[2 * K : 3 * K, :]
    coupling = jnp.concatenate([blocks[:, i : i + K] for i in range(0, 4 * TRACKS, K)], axis=0)
    p = jnp.dot(weighted, coupling, preferred_element_type=F32)
    pulled[...] = p
    total = jnp.sum(product * p, axis=0, keepdims=True)
    sent[...] = jnp.broadcast_to(total[None], sent.shape)


def later_kernel(here, za, core, chunk, got, weights, suffix, own_decay, decays):
    w = jnp.ones((1, K), F32)
    for e in range(PEERS):
        later = e > here[0]
        weights[e] = jnp.where(later, w, 0.0)
        w = jnp.where(later, w * got[(e - FIRST) % PEERS, 0:1, :], w)
    carry, keep = chunk[3], chunk[4, 0:1, :]
    f = jnp.ones((CHUNKS, K), F32)
    for i in reversed(range(STEPS)):
        decay = column(carry, i) * keep
        to = pl.ds(i, CHUNKS, stride=STEPS)
        suffix[to, :] = f
        decays[to, :] = decay
        f = decay * f
    start = pl.multiple_of((core[0] * 4 + za[0] * 2) * STEPS, QUARTER)
    for j in range(CHUNKS):
        own_decay[pl.ds(j * WIDE, FINE), :] = decays[pl.ds(start + j * FINE, FINE), :]


def sum_kernel(weights, late, own_decay, mine, other, out, p):
    for j in range(CHUNKS):
        at = pl.ds(j * FINE, FINE)
        p[pl.ds(j * WIDE, FINE), :] = mine[at, :] + other[at, :]
    r = jnp.zeros((CHUNKS, K), F32)
    m = jnp.ones((CHUNKS, K), F32)
    for i in reversed(range(FINE)):
        decay = rows(own_decay, i, WIDE)
        r = decay * (rows(p, i, WIDE) + r)
        m = decay * m
    entries = [jnp.zeros((1, K), F32)]
    for j in reversed(range(CHUNKS)):
        entries.append(m[j : j + 1] * entries[-1] + r[j : j + 1])
    total = entries.pop()
    r = jnp.concatenate(entries[::-1], axis=0)
    for i in reversed(range(FINE)):
        adjoint = rows(p, i, WIDE) + r
        out[pl.ds(i, CHUNKS, stride=FINE), :] = adjoint
        r = rows(own_decay, i, WIDE) * adjoint
    late = late[...]
    entry = jnp.sum(weights[...] * (late[:, 0:1, :] + late[:, 1:2, :]), axis=0)
    out[QUARTER:PART, :] = jnp.concatenate(
        [total, entry, jnp.zeros((PART - QUARTER - 2, K), F32)], axis=0
    )


def finish_kernel(za, d, chunk, suffix, mine, other, out_hbm, out, sems):
    gain = chunk[5, 0:1, :]
    tail = (mine[0, QUARTER:PART, :] + mine[1, QUARTER:PART, :]) + (
        other[0, QUARTER:PART, :] + other[1, QUARTER:PART, :]
    )
    entry = tail[1:2]
    copies = []
    for quarter in reversed(range(4)):
        own = za[0] == quarter % 2

        def part(at):
            return jnp.where(own, mine[quarter // 2, at, :], other[quarter // 2, at, :])

        for j in (1, 0):
            at = pl.ds((quarter * 2 + j) * STEPS, STEPS)
            entering = entry if j else chunk[0, quarter * 2 + 1 : quarter * 2 + 2, :] * entry
            adjoint = part(pl.ds(j * STEPS, STEPS)) + suffix[at, :] * entering
            out[at, :] = gain * adjoint + d[at, :].astype(F32)
            sem = sems.at[quarter * 2 + j]
            copies.append(pltpu.make_async_copy(out.at[at, :], out_hbm.at[at, :], sem))
            copies[-1].start()
        entry = chunk[0, quarter * 2 : quarter * 2 + 1, :] * entering + part(pl.ds(QUARTER, 8))[0:1]
    for copy in copies:
        copy.wait()


def local(x, d, coupling, assay, shift, span, carry, begin):
    here = lax.axis_index(BINS)[None]
    za, core = lax.axis_index("za")[None], lax.axis_index("core")[None]
    span = span.reshape(1, K)
    carry = carry.reshape(CHUNKS, STEPS)
    wide, quarter = ((ROWS, K), F32), ((QUARTER, K), F32)
    pad = VMEM((CHUNKS * PAD, K), F32)
    chunk, sent, shard = call(
        ends_kernel,
        [SMEM] + [HBM] * 7,
        [((6, CHUNKS, K), F32), ((PEERS, 3, K), F32), ((SHARD, K), F32)],
        [
            SMEM((3,), jnp.int32),
            VMEM((1, K), F32),
            VMEM((CHUNKS, STEPS), F32),
            VMEM((TRACKS // K, K), jnp.int32),
            VMEM((TRACKS, K), BF16),
            VMEM((ROWS, K), BF16),
            VMEM((ROWS, K), BF16),
            VMEM((SHARD, K), F32),
            pad,
            pad,
            pltpu.SemaphoreType.DMA((8,)),
        ],
        vmem=60,
        spaces=[VMEM, VMEM, HBM],
    )(here, begin, span, carry, assay.reshape(TRACKS // K, K), coupling, x, d)
    got = lax.all_to_all(sent, BINS, 0, 0, axis_index_groups=[ORDER], tiled=True)

    swap = [(0, 1), (1, 0)]
    other = lax.ppermute(shard, "za", swap)
    latent, moved, product, shift_t, mine = call(
        prepare_kernel,
        [SMEM] * 2 + [VMEM] * 5,
        [quarter, quarter, quarter, ((QUARTER, K), BF16), ((SHARD, K), F32)],
        [VMEM(*quarter)] * 2,
    )(za, core, chunk, x, d, shift, shard)
    (both,) = call(couple_kernel, [VMEM] * 2, [((3 * K, 4 * TRACKS), BF16)])(
        *(lax.all_gather(s, "core") for s in (mine, other))
    )

    pulled, sent = call(
        tracks_kernel,
        [SMEM] + [VMEM] * 6,
        [quarter, ((2 * PEERS, 1, K), F32)],
        vmem=32,
    )(here, got, latent, moved, product, shift_t, both)
    late = lax.all_to_all(sent, (BINS, "zb"), 0, 0, tiled=True)
    received = lax.ppermute(pulled, "zb", swap)
    weights, suffix, own_decay = call(
        later_kernel,
        [SMEM] * 3 + [VMEM] * 2,
        [((PEERS, 1, K), F32), wide, ((CHUNKS * WIDE, K), F32)],
        [VMEM(*wide)],
    )(here, za, core, chunk, got)
    (part,) = call(sum_kernel, [VMEM] * 5, [((PART, K), F32)], [VMEM((CHUNKS * WIDE, K), F32)])(
        weights, late.reshape(PEERS, 2, K), own_decay, pulled, received
    )
    other = lax.ppermute(part, "za", swap)
    mine = lax.all_gather(part, "core")
    other = lax.all_gather(other, "core")
    scratch = [VMEM(*wide), pltpu.SemaphoreType.DMA((CHUNKS,))]
    (out,) = call(finish_kernel, [SMEM] + [VMEM] * 5, [wide], scratch, spaces=[HBM])(
        za, d, chunk, suffix, mine, other
    )
    return out


def solution(mesh):
    fine = Mesh(mesh.devices.reshape(PEERS, 2, 2, 2), (BINS, *VIEW))
    in_specs = (
        P(BINS, None),
        P(BINS, None),
        P(VIEW, None),
        P(VIEW),
        P(None, BINS),
        P(),
        P(BINS),
        P(),
    )
    return jax.shard_map(
        local, mesh=fine, in_specs=in_specs, out_specs=P(BINS, None), check_vma=False
    )
```

```python
import jax
import jax.numpy as jnp
from jax import lax
from jax.experimental import pallas as pl
from jax.experimental.pallas import tpu as pltpu
from jax.sharding import Mesh, PartitionSpec as P

ROWS, QUARTER, K, CHUNKS, STEPS = 1024, 256, 128, 8, 128
PEERS, NVIEW, TRACKS = 64, 8, 640
SHARD = TRACKS + 8
FINE = 32
WIDE = FINE + 8
PAD = STEPS + 8
PART = QUARTER + 8
BINS, VIEW = "bins", ("zb", "za", "core")
FIRST = 34
ORDER = [(FIRST + i) % PEERS for i in range(PEERS)]
VMEM, SMEM, HBM = pltpu.VMEM, pltpu.SMEM, pltpu.HBM
F32, BF16 = jnp.float32, jnp.bfloat16


def spec(space):
    return pl.BlockSpec(memory_space=space)


def call(body, ins, outs, scratch=(), vmem=16, spaces=None):
    return pl.pallas_call(
        body,
        in_specs=[spec(s) for s in ins],
        out_specs=[spec(s) for s in spaces or [VMEM] * len(outs)],
        out_shape=[jax.ShapeDtypeStruct(shape, dtype) for shape, dtype in outs],
        scratch_shapes=list(scratch),
        compiler_params=pltpu.CompilerParams(vmem_limit_bytes=vmem * 1024 * 1024),
    )


def gains(span):
    forget = 1.0 / span
    return 1.0 - forget, jnp.sqrt(forget * (2.0 - forget))


def masked(carry, first, begin_ref):
    m = carry.shape[1]
    at = (
        first
        + lax.broadcasted_iota(jnp.int32, carry.shape, 0) * m
        + lax.broadcasted_iota(jnp.int32, carry.shape, 1)
    )
    begins = (at == begin_ref[0]) | (at == begin_ref[1]) | (at == begin_ref[2])
    return jnp.where(begins, 0.0, carry)


def column(carry, i):
    return jnp.broadcast_to(carry[:, i : i + 1], (CHUNKS, K))


def rows(ref, i, stride):
    return ref[pl.ds(i, CHUNKS, stride=stride), :]


def ends_kernel(
    here, begin_hbm, span_hbm, carry_hbm, assay_hbm, coupling_hbm, x_hbm, d_hbm,
    chunk, sent, shard_hbm,
    begin, span, carry_ref, assay, coupling, x, d, shard, xs, ds, sems,
):
    pairs = [
        (coupling_hbm, coupling),
        (assay_hbm, assay),
        (carry_hbm, carry_ref),
        (span_hbm, span),
        (begin_hbm, begin),
        (x_hbm, x),
        (d_hbm, d),
    ]
    copies = [pltpu.make_async_copy(a, b, sems.at[i]) for i, (a, b) in enumerate(pairs)]
    for copy in copies:
        copy.start()
    copies[0].wait()
    copies[1].wait()
    rest = jnp.zeros((SHARD - TRACKS - TRACKS // K, K), jnp.int32)
    shard[0:TRACKS, :] = coupling[...].astype(F32)
    shard[TRACKS:SHARD, :] = jnp.concatenate([assay[...], rest], axis=0).astype(F32)
    leave = pltpu.make_async_copy(shard, shard_hbm, sems.at[len(pairs)])
    leave.start()
    for copy in copies[2:]:
        copy.wait()
    keep, gain = gains(span[...])
    carry = masked(carry_ref[...], here[0] * ROWS, begin)
    for j in range(CHUNKS):
        at, to = pl.ds(j * STEPS, STEPS), pl.ds(j * PAD, STEPS)
        xs[to, :] = gain * x[at, :].astype(F32)
        ds[to, :] = gain * d[at, :].astype(F32)
    chunk[3] = carry
    chunk[4] = jnp.broadcast_to(keep, (CHUNKS, K))
    chunk[5] = jnp.broadcast_to(gain, (CHUNKS, K))
    half = STEPS // 2
    ends = []
    for first in (0, half):
        z, v = rows(xs, first, PAD), rows(ds, first, PAD)
        m = column(carry, first) * keep
        for i in range(first + 1, first + half):
            decay = column(carry, i) * keep
            z = decay * z + rows(xs, i, PAD)
            v = decay * v + rows(ds, i, PAD)
            m = decay * m
        ends.append((m, z, v))
    (m0, z0, v0), (m1, z1, v1) = ends
    m, z, v = m0 * m1, m1 * z0 + z1, m1 * v0 + v1
    chunk[0] = m
    chunk[1] = z
    chunk[2] = v
    mt, zt, vt = m[0:1], z[0:1], v[0:1]
    for j in range(1, CHUNKS):
        mj = m[j : j + 1]
        mt, zt, vt = mj * mt, mj * zt + z[j : j + 1], mj * vt + v[j : j + 1]
    sent[...] = jnp.broadcast_to(jnp.concatenate([mt, zt, vt], axis=0)[None], sent.shape)
    leave.wait()


def prepare_kernel(
    za, core, chunk, x, d, shift, shard, latent, moved, product, shift_t, mine, xs, ds
):
    mine[...] = shard[...]
    at = core[0] * 4 + za[0] * 2
    start = pl.multiple_of(at * STEPS, QUARTER)
    pair, keep, gain = chunk[3, pl.ds(at, 2), :], chunk[4, 0:1, :], chunk[5, 0:1, :]
    carry = jnp.concatenate(
        [pair[j : j + 1, i : i + FINE] for j in range(2) for i in range(0, STEPS, FINE)], axis=0
    )
    xs[...] = gain * x[pl.ds(start, QUARTER), :].astype(F32)
    ds[...] = gain * d[pl.ds(start, QUARTER), :].astype(F32)
    z, v = rows(xs, 0, FINE), rows(ds, 0, FINE)
    m = column(carry, 0) * keep
    for i in range(1, FINE):
        decay = column(carry, i) * keep
        z = decay * z + rows(xs, i, FINE)
        v = decay * v + rows(ds, i, FINE)
        m = decay * m
    q, ez, ev = jnp.ones((1, K), F32), jnp.zeros((1, K), F32), jnp.zeros((1, K), F32)
    for j in range(CHUNKS - 2):
        before = j < at
        mj, zj, vj = (chunk[i, j : j + 1, :] for i in range(3))
        q = jnp.where(before, mj * q, q)
        ez = jnp.where(before, mj * ez + zj, ez)
        ev = jnp.where(before, mj * ev + vj, ev)
    qs, zs, vs = [q], [ez], [ev]
    for j in range(CHUNKS - 1):
        mj = m[j : j + 1]
        qs.append(mj * qs[-1])
        zs.append(mj * zs[-1] + z[j : j + 1])
        vs.append(mj * vs[-1] + v[j : j + 1])
    q, z, v = (jnp.concatenate(a, axis=0) for a in (qs, zs, vs))
    for i in range(FINE):
        decay = column(carry, i) * keep
        q = decay * q
        z = decay * z + rows(xs, i, FINE)
        v = decay * v + rows(ds, i, FINE)
        to = pl.ds(i, CHUNKS, stride=FINE)
        product[to, :] = q
        latent[to, :] = z
        moved[to, :] = v
    s = shift[:, pl.ds(start, QUARTER)]
    hi = s.astype(BF16).astype(F32)
    mid = (s - hi).astype(BF16).astype(F32)
    low = s - hi - mid
    blank = jnp.zeros((K - 3 * NVIEW, QUARTER), F32)
    shift_t[...] = jnp.concatenate([hi, mid, low, blank], axis=0).T.astype(BF16)


def couple_kernel(mine, other, both):
    for side in range(4):
        ref = (mine, other)[side // 2].at[side % 2]
        at = pl.ds(side * TRACKS, TRACKS)
        w = ref[0:TRACKS, :]
        both[0:K, at] = w.T.astype(BF16)
        both[2 * K : 3 * K, at] = jnp.concatenate(
            [w[i : i + K] for i in range(0, TRACKS, K)], axis=1
        ).astype(BF16)
        assay = ref[TRACKS:SHARD, :]
        assay = jnp.concatenate([assay[i : i + 1] for i in range(TRACKS // K)], axis=1)
        view = lax.broadcasted_iota(jnp.int32, (NVIEW, TRACKS), 0).astype(F32)
        member = (assay == view).astype(F32)
        blank = jnp.zeros((K - 3 * NVIEW, TRACKS), F32)
        both[K : 2 * K, at] = jnp.concatenate([member] * 3 + [blank], axis=0).astype(BF16)


def tracks_kernel(
    here, got, latent_ref, moved_ref, product_ref, shift_t, both,
    pulled, sent,
):
    ez = jnp.zeros((1, K), F32)
    ev = jnp.zeros((1, K), F32)
    for e in range(PEERS - 1):
        at = (e - FIRST) % PEERS
        m, z, v = got[at, 0:1, :], got[at, 1:2, :], got[at, 2:3, :]
        earlier = e < here[0]
        ez = jnp.where(earlier, m * ez + z, ez)
        ev = jnp.where(earlier, m * ev + v, ev)
    product = product_ref[...]
    latent = (latent_ref[...] + product * ez).astype(BF16)
    latent = jnp.concatenate([latent, shift_t[...]], axis=1)
    moved = (moved_ref[...] + product * ev).astype(BF16)
    log_rate = jnp.dot(latent, both[0 : 2 * K, :], preferred_element_type=F32)
    along = jnp.dot(moved, both[0:K, :], preferred_element_type=F32)
    weighted = (jnp.exp(log_rate) * along).astype(BF16)
    blocks = both[2 * K : 3 * K, :]
    coupling = jnp.concatenate([blocks[:, i : i + K] for i in range(0, 4 * TRACKS, K)], axis=0)
    p = jnp.dot(weighted, coupling, preferred_element_type=F32)
    pulled[...] = p
    total = jnp.sum(product * p, axis=0, keepdims=True)
    sent[...] = jnp.broadcast_to(total[None], sent.shape)


def later_kernel(here, za, core, chunk, got, weights, suffix, own_decay, decays):
    w = jnp.ones((1, K), F32)
    for e in range(PEERS):
        later = e > here[0]
        weights[e] = jnp.where(later, w, 0.0)
        w = jnp.where(later, w * got[(e - FIRST) % PEERS, 0:1, :], w)
    carry, keep = chunk[3], chunk[4, 0:1, :]
    f = jnp.ones((CHUNKS, K), F32)
    for i in reversed(range(STEPS)):
        decay = column(carry, i) * keep
        to = pl.ds(i, CHUNKS, stride=STEPS)
        suffix[to, :] = f
        decays[to, :] = decay
        f = decay * f
    start = pl.multiple_of((core[0] * 4 + za[0] * 2) * STEPS, QUARTER)
    for j in range(CHUNKS):
        own_decay[pl.ds(j * WIDE, FINE), :] = decays[pl.ds(start + j * FINE, FINE), :]


def sum_kernel(weights, late, own_decay, mine, other, out, p):
    for j in range(CHUNKS):
        at = pl.ds(j * FINE, FINE)
        p[pl.ds(j * WIDE, FINE), :] = mine[at, :] + other[at, :]
    r = jnp.zeros((CHUNKS, K), F32)
    m = jnp.ones((CHUNKS, K), F32)
    for i in reversed(range(FINE)):
        decay = rows(own_decay, i, WIDE)
        r = decay * (rows(p, i, WIDE) + r)
        m = decay * m
    entries = [jnp.zeros((1, K), F32)]
    for j in reversed(range(CHUNKS)):
        entries.append(m[j : j + 1] * entries[-1] + r[j : j + 1])
    total = entries.pop()
    r = jnp.concatenate(entries[::-1], axis=0)
    for i in reversed(range(FINE)):
        adjoint = rows(p, i, WIDE) + r
        out[pl.ds(i, CHUNKS, stride=FINE), :] = adjoint
        r = rows(own_decay, i, WIDE) * adjoint
    late = late[...]
    entry = jnp.sum(weights[...] * (late[:, 0:1, :] + late[:, 1:2, :]), axis=0)
    out[QUARTER:PART, :] = jnp.concatenate(
        [total, entry, jnp.zeros((PART - QUARTER - 2, K), F32)], axis=0
    )


def finish_kernel(za, d, chunk, suffix, mine, other, out):
    gain = chunk[5, 0:1, :]
    tail = (mine[0, QUARTER:PART, :] + mine[1, QUARTER:PART, :]) + (
        other[0, QUARTER:PART, :] + other[1, QUARTER:PART, :]
    )
    entry = tail[1:2]
    for quarter in reversed(range(4)):
        own = za[0] == quarter % 2

        def part(at):
            return jnp.where(own, mine[quarter // 2, at, :], other[quarter // 2, at, :])

        for j in (1, 0):
            at = pl.ds((quarter * 2 + j) * STEPS, STEPS)
            entering = entry if j else chunk[0, quarter * 2 + 1 : quarter * 2 + 2, :] * entry
            adjoint = part(pl.ds(j * STEPS, STEPS)) + suffix[at, :] * entering
            out[at, :] = gain * adjoint + d[at, :].astype(F32)
        entry = chunk[0, quarter * 2 : quarter * 2 + 1, :] * entering + part(pl.ds(QUARTER, 8))[0:1]


def local(x, d, coupling, assay, shift, span, carry, begin):
    here = lax.axis_index(BINS)[None]
    za, core = lax.axis_index("za")[None], lax.axis_index("core")[None]
    span = span.reshape(1, K)
    carry = carry.reshape(CHUNKS, STEPS)
    wide, quarter = ((ROWS, K), F32), ((QUARTER, K), F32)
    pad = VMEM((CHUNKS * PAD, K), F32)
    chunk, sent, shard = call(
        ends_kernel,
        [SMEM] + [HBM] * 7,
        [((6, CHUNKS, K), F32), ((PEERS, 3, K), F32), ((SHARD, K), F32)],
        [
            SMEM((3,), jnp.int32),
            VMEM((1, K), F32),
            VMEM((CHUNKS, STEPS), F32),
            VMEM((TRACKS // K, K), jnp.int32),
            VMEM((TRACKS, K), BF16),
            VMEM((ROWS, K), BF16),
            VMEM((ROWS, K), BF16),
            VMEM((SHARD, K), F32),
            pad,
            pad,
            pltpu.SemaphoreType.DMA((8,)),
        ],
        vmem=60,
        spaces=[VMEM, VMEM, HBM],
    )(here, begin, span, carry, assay.reshape(TRACKS // K, K), coupling, x, d)
    got = lax.all_to_all(sent, BINS, 0, 0, axis_index_groups=[ORDER], tiled=True)

    swap = [(0, 1), (1, 0)]
    other = lax.ppermute(shard, "za", swap)
    latent, moved, product, shift_t, mine = call(
        prepare_kernel,
        [SMEM] * 2 + [VMEM] * 5,
        [quarter, quarter, quarter, ((QUARTER, K), BF16), ((SHARD, K), F32)],
        [VMEM(*quarter)] * 2,
    )(za, core, chunk, x, d, shift, shard)
    (both,) = call(couple_kernel, [VMEM] * 2, [((3 * K, 4 * TRACKS), BF16)])(
        *(lax.all_gather(s, "core") for s in (mine, other))
    )

    pulled, sent = call(
        tracks_kernel,
        [SMEM] + [VMEM] * 6,
        [quarter, ((2 * PEERS, 1, K), F32)],
        vmem=32,
    )(here, got, latent, moved, product, shift_t, both)
    late = lax.all_to_all(sent, (BINS, "zb"), 0, 0, tiled=True)
    received = lax.ppermute(pulled, "zb", swap)
    weights, suffix, own_decay = call(
        later_kernel,
        [SMEM] * 3 + [VMEM] * 2,
        [((PEERS, 1, K), F32), wide, ((CHUNKS * WIDE, K), F32)],
        [VMEM(*wide)],
    )(here, za, core, chunk, got)
    (part,) = call(sum_kernel, [VMEM] * 5, [((PART, K), F32)], [VMEM((CHUNKS * WIDE, K), F32)])(
        weights, late.reshape(PEERS, 2, K), own_decay, pulled, received
    )
    other = lax.ppermute(part, "za", swap)
    mine = lax.all_gather(part, "core")
    other = lax.all_gather(other, "core")
    (out,) = call(finish_kernel, [SMEM] + [VMEM] * 5, [wide])(
        za, d, chunk, suffix, mine, other
    )
    return out


def solution(mesh):
    fine = Mesh(mesh.devices.reshape(PEERS, 2, 2, 2), (BINS, *VIEW))
    in_specs = (
        P(BINS, None),
        P(BINS, None),
        P(VIEW, None),
        P(VIEW),
        P(None, BINS),
        P(),
        P(BINS),
        P(),
    )
    return jax.shard_map(
        local, mesh=fine, in_specs=in_specs, out_specs=P(BINS, None), check_vma=False
    )
```
